512 devices in a mesh: rows: 128 (over z, x, core), cols: 4 (over y).
Axes of the slice: x: 4, y: 4, z: 16, core: 2. Of those that a mesh axis runs over, the one named last changes fastest.
Arguments:
- gradients: bfloat16 [98304, 8192], P('rows', 'cols'), may hold values from -60 to 60, as said below
- projection: bfloat16 [8192, 256], P('cols'), may hold values from -0.0625 to 0.0625
Outputs:
- basis: float32 [98304, 256], P('rows')
- reduced: float32 [256, 8192], P('rows', 'cols')
The draws below stay inside these ranges and needn't reach their ends.
Inputs may be any that keep to these rules, and one draw needn't show every extreme that they name: Real-valued gradients; entries independent given per-example and per-feature scales.
All inputs are finite; a program needn't handle non-finite values.
Results may differ from the reference program's by a relative error of at most 0.0012.
Values sent between devices are 32-bit elements; how exact they have to be, the bound alone decides.
No kernel may reach another device: no remote copies, remote signals or barrier semaphores. Data moves between devices by JAX's collectives and lax.ppermute only.
A program may use at most 64 MiB of HBM per device.

```python
import jax
import jax.numpy as jnp
from jax import lax

FEAT = 8192
RANK = 256
ROWS = 98304


def draw_gradients(key, part):
    key = jax.random.fold_in(key, 11)
    key_rows, key_cols, key_base = jax.random.split(key, 3)
    row_power = jax.random.uniform(key_rows, (ROWS, 1), dtype=jnp.float32)
    col_power = jax.random.uniform(key_cols, (1, FEAT), dtype=jnp.float32)
    position = jnp.arange(ROWS, dtype=jnp.float32)[:, None] / ROWS
    base = jnp.clip(jax.random.normal(key_base, (ROWS, FEAT), dtype=jnp.float32), -4.0, 4.0)
    trend = 3.0 ** position
    values = 0.05 * base * 10.0 ** row_power * 10.0 ** col_power * trend
    return values.astype(jnp.bfloat16)


def level_of(stream_key, extent, pieces, smallest, largest):
    loudness = 1.0
    for dim, blocks in pieces:
        steps = jax.random.uniform(jax.random.fold_in(jax.random.fold_in(stream_key, 6), dim), (blocks,), jnp.float32, smallest / len(pieces), largest / len(pieces))
        loudness = loudness * jnp.repeat(jnp.exp(steps), extent[dim] // blocks).reshape((-1,) + (1,) * (len(extent) - 1 - dim))
    return loudness


def bell_draw(stream_key, shape, scale, reach, shards=(), kind=jnp.bfloat16):
    result = scale * jax.random.normal(stream_key, shape, jnp.float32)
    if shards:
        result = result * level_of(stream_key, shape, shards, -0.22, 0.18)
    return jnp.clip(result, -reach, reach).astype(kind)


def setup_inputs(seed: int = 0) -> dict:
    key_list = jax.random.split(jax.random.key(seed), 3)
    return {
        "gradients": draw_gradients(jax.random.fold_in(key_list[2], 71), 0),
        "projection": bell_draw(key_list[1], (FEAT, RANK), FEAT ** -0.5, 0.0625, ((0, 4),)),
    }


def reference(gradients, projection):
    sketch = jnp.dot(gradients.astype(jnp.float32), projection.astype(jnp.float32), preferred_element_type=jnp.float32)
    gram = jnp.dot(sketch.T, sketch, precision=lax.Precision.HIGHEST)
    lower = jnp.linalg.cholesky(gram)
    factor = float(ROWS) ** 0.5
    basis = jax.scipy.linalg.solve_triangular(lower, sketch.T, lower=True).T * factor
    half = sketch.astype(jnp.bfloat16)
    moment = jnp.dot(half.T.astype(jnp.float32), gradients.astype(jnp.float32), preferred_element_type=jnp.float32)
    reduced = jax.scipy.linalg.solve_triangular(lower, moment, lower=True)
    return (basis, reduced)
```

```python
import jax
import jax.numpy as jnp
from jax import lax
from jax.sharding import Mesh
from jax.sharding import PartitionSpec as P

HIGHEST = lax.Precision.HIGHEST
ROWS = ("z", "x", "core")
NEAR = ("x", "core", "y")


def exchange(blocks, axes):
    return lax.all_to_all(blocks, axes, 0, 0)


def spread(block, axes):
    count = lax.axis_size(axes)
    return exchange(jnp.broadcast_to(block[None], (count, *block.shape)), axes)


def on_device(gradients, projection):
    rows, feats = gradients.shape
    rank = projection.shape[1]
    total_rows = rows * lax.axis_size(ROWS)
    factor = float(total_rows) ** 0.5

    with jax.named_scope("sketch"):
        partial = jnp.dot(gradients, projection, preferred_element_type=jnp.float32)
        groups = lax.axis_size("y")
        own = exchange(partial.reshape(groups, rows // groups, rank), "y").sum(0)
        sketch = spread(own, "y").reshape(rows, rank)

    with jax.named_scope("gram"):
        local = jnp.dot(own.T, own, precision=HIGHEST)
        near = lax.axis_size(NEAR)
        share = exchange(local.reshape(near, rank // near, rank), NEAR).sum(0)
        share = spread(share, "z").sum(0)
        gram = spread(share, NEAR).reshape(rank, rank)

    with jax.named_scope("factor"):
        lower = jnp.linalg.cholesky(gram)
        inverse = jax.scipy.linalg.solve_triangular(
            lower, jnp.eye(rank, dtype=jnp.float32), lower=True
        )

    with jax.named_scope("moment"):
        half = sketch.astype(jnp.bfloat16)
        cores, xs = lax.axis_size("core"), lax.axis_size("x")
        width = feats // (cores * xs)
        moment = jnp.stack(
            [
                jnp.einsum(
                    "rk,rf->kf",
                    half,
                    gradients[:, i * width : (i + 1) * width],
                    preferred_element_type=jnp.float32,
                )
                for i in range(cores * xs)
            ]
        ).reshape(cores, xs, rank, width)
        core = lax.axis_index("core")
        away = lax.dynamic_index_in_dim(moment, 1 - core, 0, keepdims=False)
        here = lax.dynamic_index_in_dim(moment, core, 0, keepdims=False)
        moment = here + lax.ppermute(away, "core", [(0, 1), (1, 0)])
        moment = exchange(moment, "x").sum(0)

    with jax.named_scope("reduced"):
        solved = jnp.dot(inverse, moment, precision=HIGHEST)
        members = lax.axis_size(ROWS)
        parts = exchange(solved.reshape(members, rank // members, width), ROWS)
        parts = parts.reshape(lax.axis_size("z"), xs, cores, rank // members, width).sum(0)
        reduced = parts.transpose(2, 1, 0, 3).reshape(rank // members, feats)

    with jax.named_scope("basis"):
        basis = jnp.dot(sketch, inverse.T, precision=HIGHEST) * factor
    return (basis, reduced)


def solution(mesh):
    devices = mesh.devices.reshape(16, 4, 2, 4)
    fine = Mesh(devices, ("z", "x", "core", "y"))
    in_specs = (P(ROWS, "y"), P("y", None))
    out_specs = (P(ROWS, None), P(ROWS, "y"))
    return jax.shard_map(
        on_device, mesh=fine, in_specs=in_specs, out_specs=out_specs, check_vma=False
    )
```

```python
import jax
import jax.numpy as jnp
from jax import lax
from jax.experimental import pallas as pl
from jax.experimental.pallas import tpu as pltpu
from jax.sharding import Mesh
from jax.sharding import PartitionSpec as P

HIGHEST = lax.Precision.HIGHEST
ROWS = ("z", "x", "core")
NEAR = ("x", "core", "y")
PANEL = 8
VMEM_LIMIT = 32 * 1024 * 1024


def exchange(blocks, axes):
    return lax.all_to_all(blocks, axes, 0, 0)


def spread(block, axes):
    count = lax.axis_size(axes)
    return exchange(jnp.broadcast_to(block[None], (count, *block.shape)), axes)


def dot(a, b, contract):
    return lax.dot_general(
        a,
        b,
        (contract, ((), ())),
        precision=HIGHEST,
        preferred_element_type=jnp.float32,
    )


def inverse_factor(square):
    n = square.shape[0]
    count = n // PANEL
    sub = lax.broadcasted_iota(jnp.int32, (PANEL, n), 0)
    lane = lax.broadcasted_iota(jnp.int32, (PANEL, n), 1)

    def wide(part):
        return jnp.broadcast_to(part, (PANEL, n))

    left = [square[PANEL * i : PANEL * (i + 1), :] for i in range(count)]
    right = [jnp.where(lane == sub + PANEL * i, 1.0, 0.0) for i in range(count)]
    done = []
    for k in range(count):
        columns = [
            [wide(left[i][:, PANEL * k + j : PANEL * k + j + 1]) for i in range(k, count)]
            for j in range(PANEL)
        ]
        pivots = None
        for j in range(PANEL):
            pivot = wide(columns[j][0][j : j + 1, :])
            pivots = pivot if pivots is None else jnp.where(sub == j, pivot, pivots)
            inverse = 1.0 / pivot
            left_row = wide(left[k][j : j + 1, :])
            right_row = wide(right[k][j : j + 1, :])
            later = [wide(columns[m][0][j : j + 1, :]) for m in range(j + 1, PANEL)]
            for i in range(k, count):
                if i == k and j == PANEL - 1:
                    continue
                scale = columns[j][i - k] * inverse
                if i == k:
                    scale = jnp.where(sub > j, scale, 0.0)
                left[i] = left[i] - scale * left_row
                right[i] = right[i] - scale * right_row
                for m in range(j + 1, PANEL):
                    columns[m][i - k] = columns[m][i - k] - scale * later[m - j - 1]
        done.append(right[k] * lax.rsqrt(pivots))
    return jnp.concatenate(done, 0)


def factor_kernel(gram, out):
    n = gram.shape[0] // 2
    top = inverse_factor(gram[:n, :n])
    low = dot(gram[n:, :n], top, ((1,), (1,)))
    bottom = inverse_factor(gram[n:, n:] - dot(low, low, ((1,), (1,))))
    out[:n, :n] = top
    out[:n, n:] = jnp.zeros((n, n), jnp.float32)
    out[n:, n:] = bottom
    out[n:, :n] = -dot(bottom, dot(low, top, ((1,), (0,))), ((1,), (0,)))


def factor(gram):
    return pl.pallas_call(
        factor_kernel,
        out_shape=jax.ShapeDtypeStruct(gram.shape, jnp.float32),
        in_specs=[pl.BlockSpec(memory_space=pltpu.VMEM)],
        out_specs=pl.BlockSpec(memory_space=pltpu.VMEM),
        compiler_params=pltpu.CompilerParams(vmem_limit_bytes=VMEM_LIMIT),
        cost_estimate=pl.CostEstimate(
            flops=10**10, bytes_accessed=2 * gram.size * 4, transcendentals=0
        ),
        name="factor",
    )(gram)


def moment_kernel(side, half, gradients, *refs):
    value = lax.dot_general(
        half[...],
        gradients[...],
        (((0,), (0,)), ((), ())),
        preferred_element_type=jnp.float32,
    )
    if len(refs) == 2:
        value = value + refs[0][0]
    refs[-1][0] = value


def moment_blocks(half, gradients, side, blocks, added=None):
    rows, rank = half.shape
    width = gradients.shape[1] // (2 * blocks)
    block = pl.BlockSpec((1, rank, width), lambda i, side: (i, 0, 0))
    return pl.pallas_call(
        moment_kernel,
        out_shape=jax.ShapeDtypeStruct((blocks, rank, width), jnp.float32),
        grid_spec=pltpu.PrefetchScalarGridSpec(
            num_scalar_prefetch=1,
            grid=(blocks,),
            in_specs=[
                pl.BlockSpec((rows, rank), lambda i, side: (0, 0)),
                pl.BlockSpec((rows, width), lambda i, side: (0, side[0] * blocks + i)),
            ]
            + ([] if added is None else [block]),
            out_specs=block,
        ),
        compiler_params=pltpu.CompilerParams(vmem_limit_bytes=VMEM_LIMIT),
        cost_estimate=pl.CostEstimate(
            flops=2 * rows * rank * width * blocks,
            bytes_accessed=rows * width * blocks * 2 + rank * width * blocks * 4,
            transcendentals=0,
        ),
        name="moment",
    )(*([side, half, gradients] + ([] if added is None else [added])))


def on_device(gradients, projection):
    rows, feats = gradients.shape
    rank = projection.shape[1]
    scale = float(rows * lax.axis_size(ROWS)) ** 0.5
    cores, xs = lax.axis_size("core"), lax.axis_size("x")
    core = lax.axis_index("core").astype(jnp.int32)

    with jax.named_scope("sketch"):
        partial = jnp.dot(gradients, projection, preferred_element_type=jnp.float32)
        groups = lax.axis_size("y")
        own = exchange(partial.reshape(groups, rows // groups, rank), "y").sum(0)
        sketch = spread(own, "y").reshape(rows, rank)

    with jax.named_scope("gram"):
        local = dot(own, own, ((0,), (0,)))
        near = lax.axis_size(NEAR)
        share = exchange(local.reshape(near, rank // near, rank), NEAR).sum(0)
        share = spread(share, "z").sum(0)
        gram = spread(share, NEAR).reshape(rank, rank)

    with jax.named_scope("factor"):
        inverse = factor(gram)

    with jax.named_scope("moment"):
        half = sketch.astype(jnp.bfloat16)
        away = moment_blocks(half, gradients, (1 - core)[None], xs)
        away = lax.ppermute(away, "core", [(0, 1), (1, 0)])
        moment = moment_blocks(half, gradients, core[None], xs, away)
        moment = exchange(moment, "x").sum(0)

    with jax.named_scope("reduced"):
        width = feats // (cores * xs)
        solved = dot(inverse, moment, ((1,), (0,)))
        members = lax.axis_size(ROWS)
        parts = exchange(solved.reshape(members, rank // members, width), ROWS)
        parts = parts.reshape(lax.axis_size("z"), xs, cores, rank // members, width).sum(0)
        reduced = parts.transpose(2, 1, 0, 3).reshape(rank // members, feats)

    with jax.named_scope("basis"):
        basis = dot(sketch, inverse, ((1,), (1,))) * scale
    return (basis, reduced)


def solution(mesh):
    devices = mesh.devices.reshape(16, 4, 2, 4)
    fine = Mesh(devices, ("z", "x", "core", "y"))
    in_specs = (P(ROWS, "y"), P("y", None))
    out_specs = (P(ROWS, None), P(ROWS, "y"))
    return jax.shard_map(
        on_device, mesh=fine, in_specs=in_specs, out_specs=out_specs, check_vma=False
    )
```

```python
import jax
import jax.numpy as jnp
from jax import lax
from jax.experimental import pallas as pl
from jax.experimental.pallas import tpu as pltpu
from jax.sharding import Mesh
from jax.sharding import PartitionSpec as P

HIGHEST = lax.Precision.HIGHEST
ROWS = ("z", "x", "core")
NEAR = ("x", "core", "y")
PANEL = 8
VMEM_LIMIT = 8 * 1024 * 1024


def exchange(blocks, axes):
    return lax.all_to_all(blocks, axes, 0, 0)


def shifted(value, axis, by):
    count = lax.axis_size(axis)
    return lax.ppermute(value, axis, [(i, (i + by) % count) for i in range(count)])


def dot(a, b, contract):
    return lax.dot_general(
        a,
        b,
        (contract, ((), ())),
        precision=HIGHEST,
        preferred_element_type=jnp.float32,
    )


def inverse_factor(square):
    n = square.shape[0]
    count = n // PANEL
    sub = lax.broadcasted_iota(jnp.int32, (PANEL, n), 0)
    lane = lax.broadcasted_iota(jnp.int32, (PANEL, n), 1)

    def wide(part):
        return jnp.broadcast_to(part, (PANEL, n))

    left = [square[PANEL * i : PANEL * (i + 1), :] for i in range(count)]
    right = [jnp.where(lane == sub + PANEL * i, 1.0, 0.0) for i in range(count)]
    done = []
    for k in range(count):
        columns = [
            [wide(left[i][:, PANEL * k + j : PANEL * k + j + 1]) for i in range(k, count)]
            for j in range(PANEL)
        ]
        pivots = None
        for j in range(PANEL):
            pivot = wide(columns[j][0][j : j + 1, :])
            pivots = pivot if pivots is None else jnp.where(sub == j, pivot, pivots)
            inverse = 1.0 / pivot
            left_row = wide(left[k][j : j + 1, :])
            right_row = wide(right[k][j : j + 1, :])
            later = [wide(columns[m][0][j : j + 1, :]) for m in range(j + 1, PANEL)]
            for i in range(k, count):
                if i == k and j == PANEL - 1:
                    continue
                scale = columns[j][i - k] * inverse
                if i == k:
                    scale = jnp.where(sub > j, scale, 0.0)
                left[i] = left[i] - scale * left_row
                right[i] = right[i] - scale * right_row
                for m in range(j + 1, PANEL):
                    columns[m][i - k] = columns[m][i - k] - scale * later[m - j - 1]
        done.append(right[k] * lax.rsqrt(pivots))
    return jnp.concatenate(done, 0)


def call(kernel, name, flops, outs, *args, after=()):
    whole = pl.BlockSpec()
    smem = pl.BlockSpec(memory_space=pltpu.SMEM)
    moved = sum(a.size * a.dtype.itemsize for a in (*args, *outs))
    return pl.pallas_call(
        lambda *refs: kernel(*refs[len(after) :]),
        out_shape=outs,
        in_specs=[pl.BlockSpec(memory_space=pl.ANY)] * len(after)
        + [smem if a.ndim == 1 else whole for a in args],
        out_specs=[whole] * len(outs),
        compiler_params=pltpu.CompilerParams(vmem_limit_bytes=VMEM_LIMIT),
        cost_estimate=pl.CostEstimate(flops=flops, bytes_accessed=moved, transcendentals=0),
        name=name,
    )(*after, *args)


def f32(*shape):
    return jax.ShapeDtypeStruct(shape, jnp.float32)


def gram_kernel(parts, own, gram):
    total = jnp.sum(parts[...], 0)
    own[...] = total
    gram[...] = dot(total, total, ((0,), (0,))).reshape(gram.shape)


def tile_kernel(parts, tiles):
    total = jnp.sum(parts[...], 0)
    for i in range(tiles.shape[0]):
        tiles[i] = total


def factor_kernel(shares, out):
    gram = shares[...].reshape(out.shape)
    n = gram.shape[0] // 2
    top = inverse_factor(gram[:n, :n])
    low = dot(gram[n:, :n], top, ((1,), (1,)))
    bottom = inverse_factor(gram[n:, n:] - dot(low, low, ((1,), (1,))))
    out[:n, :n] = top
    out[:n, n:] = jnp.zeros((n, n), jnp.float32)
    out[n:, n:] = bottom
    out[n:, :n] = -dot(bottom, dot(low, top, ((1,), (0,))), ((1,), (0,)))


def place_kernel(mine, *refs):
    sketch, half = refs[-2:]
    count = len(refs) - 2
    size = refs[0].shape[0]
    for k in range(count):
        member = lax.rem(mine[0] + count - k, count)
        rows = pl.ds(pl.multiple_of(member * size, size), size)
        block = refs[k][...]
        sketch[rows, :] = block
        half[rows, :] = block.astype(half.dtype)


def solve_kernel(inverse, *refs):
    out = refs[-1]
    total = refs[0][...]
    for part in refs[1:-1]:
        total = total + part[...]
    out[...] = dot(inverse[...], total, ((1,), (0,))).reshape(out.shape)


def sketch_kernel(gradients, projection, partial, held, weights, sems):
    blocks, size, _ = partial.shape
    first = pltpu.make_async_copy(projection, weights, sems.at[blocks])
    first.start()
    copies = []
    for i in range(blocks):
        part = pl.ds(i * size, size)
        copies.append(
            pltpu.make_async_copy(gradients.at[part], held.at[part], sems.at[i])
        )
        copies[-1].start()
    first.wait()
    for i in range(blocks):
        copies[i].wait()
        partial[i] = jnp.dot(
            held[i * size : (i + 1) * size, :],
            weights[...],
            preferred_element_type=jnp.float32,
        )


def sketch_blocks(gradients, projection, blocks):
    rows, feats = gradients.shape
    rank = projection.shape[1]
    return pl.pallas_call(
        sketch_kernel,
        out_shape=[
            f32(blocks, rows // blocks, rank),
            jax.ShapeDtypeStruct(gradients.shape, gradients.dtype),
        ],
        in_specs=[pl.BlockSpec(memory_space=pltpu.HBM)] * 2,
        out_specs=[pl.BlockSpec(), pl.BlockSpec(memory_space=pltpu.VMEM)],
        scratch_shapes=[
            pltpu.VMEM(projection.shape, projection.dtype),
            pltpu.SemaphoreType.DMA((blocks + 1,)),
        ],
        compiler_params=pltpu.CompilerParams(vmem_limit_bytes=VMEM_LIMIT),
        cost_estimate=pl.CostEstimate(
            flops=2 * rows * feats * rank,
            bytes_accessed=2 * feats * (rows + rank),
            transcendentals=0,
        ),
        name="sketch",
    )(gradients, projection)


def moment_kernel(place, half, gradients, *refs):
    count = refs[-1].shape[0] if len(refs) == 1 else len(refs) - 1
    width = gradients.shape[1] // (2 * count)
    turned = half[...].T
    for i in range(count):
        block = place[0] * count + lax.rem(place[1] + i, count)
        columns = pl.ds(pl.multiple_of(block * width, width), width)
        value = jnp.dot(turned, gradients[:, columns], preferred_element_type=jnp.float32)
        if len(refs) == 1:
            refs[0][i] = value
        else:
            refs[1 + i][...] = value + refs[0][i]


def moment_blocks(half, gradients, place, count, added=None):
    rows, rank = half.shape
    width = gradients.shape[1] // (2 * count)
    vmem, whole = pl.BlockSpec(memory_space=pltpu.VMEM), pl.BlockSpec()
    outs = [f32(count, rank, width)] if added is None else [f32(rank, width)] * count
    args = [half, gradients] + ([] if added is None else [added])
    return pl.pallas_call(
        moment_kernel,
        out_shape=outs,
        in_specs=[pl.BlockSpec(memory_space=pltpu.SMEM), vmem, vmem]
        + [whole] * (len(args) - 2),
        out_specs=[whole] * len(outs),
        compiler_params=pltpu.CompilerParams(vmem_limit_bytes=VMEM_LIMIT),
        cost_estimate=pl.CostEstimate(
            flops=2 * rows * rank * width * count,
            bytes_accessed=rows * width * count * 2 + rank * width * count * 4,
            transcendentals=0,
        ),
        name="moment",
    )(place, *args)


def on_device(gradients, projection):
    rows, feats = gradients.shape
    rank = projection.shape[1]
    scale = float(rows * lax.axis_size(ROWS)) ** 0.5
    cores, xs = lax.axis_size("core"), lax.axis_size("x")
    core = lax.axis_index("core").astype(jnp.int32)

    near, members = lax.axis_size(NEAR), lax.axis_size(ROWS)
    zs, groups = lax.axis_size("z"), lax.axis_size("y")
    width = feats // (cores * xs)

    with jax.named_scope("sketch"):
        partial, held = sketch_blocks(gradients, projection, groups)
        parts = exchange(partial, "y")

    with jax.named_scope("gram"):
        own, shares = call(
            gram_kernel,
            "gram",
            12 * rows // groups * rank**2,
            [f32(rows // groups, rank), f32(near, rank // near, rank)],
            parts,
        )
        shares = exchange(shares, NEAR)

    with jax.named_scope("gather"):
        others = [shifted(own, "y", k) for k in range(1, groups)]
        mine = lax.axis_index("y").astype(jnp.int32)[None]
        sketch, half = call(
            place_kernel,
            "place",
            0,
            [f32(rows, rank), jax.ShapeDtypeStruct((rows, rank), jnp.bfloat16)],
            mine,
            own,
            *others,
            after=[shares],
        )

    with jax.named_scope("gram"):
        (shares,) = call(tile_kernel, "tile", 0, [f32(zs, rank // near, rank)], shares)
        shares = exchange(shares, "z")
        (shares,) = call(tile_kernel, "tile", 0, [f32(near, rank // near, rank)], shares)
        shares = exchange(shares, NEAR)

    with jax.named_scope("factor"):
        (inverse,) = call(factor_kernel, "factor", 10**10, [f32(rank, rank)], shares)

    with jax.named_scope("moment"):
        x = lax.axis_index("x").astype(jnp.int32)
        away = moment_blocks(half, held, jnp.stack([1 - core, x]), xs)[0]
        away = lax.ppermute(away, "core", [(0, 1), (1, 0)])
        moment = moment_blocks(half, held, jnp.stack([core, x]), xs, away)
        moment = [moment[0]] + [shifted(moment[k], "x", k) for k in range(1, xs)]

    with jax.named_scope("reduced"):
        (parts,) = call(
            solve_kernel,
            "solve",
            12 * rank**2 * width,
            [f32(members, rank // members, width)],
            inverse,
            *moment,
        )
        parts = exchange(parts, ROWS)
        parts = parts.reshape(zs, xs, cores, rank // members, width).sum(0)
        reduced = parts.transpose(2, 1, 0, 3).reshape(rank // members, feats)

    with jax.named_scope("basis"):
        basis = dot(sketch, inverse, ((1,), (1,))) * scale
    return (basis, reduced)


def solution(mesh):
    devices = mesh.devices.reshape(16, 4, 2, 4)
    fine = Mesh(devices, ("z", "x", "core", "y"))
    in_specs = (P(ROWS, "y"), P("y", None))
    out_specs = (P(ROWS, None), P(ROWS, "y"))
    return jax.shard_map(
        on_device, mesh=fine, in_specs=in_specs, out_specs=out_specs, check_vma=False
    )
```

```python
import math

import jax
import jax.numpy as jnp
from jax import lax
from jax.experimental import pallas as pl
from jax.experimental.pallas import tpu as pltpu
from jax.sharding import Mesh
from jax.sharding import PartitionSpec as P

HIGHEST = lax.Precision.HIGHEST
ROWS = ("z", "x", "core")
NEAR = ("x", "core", "y")
PANEL = 8
SHORT = 3 * 10**10
VMEM_LIMIT = 8 * 1024 * 1024


def exchange(blocks, axes):
    return lax.all_to_all(blocks, axes, 0, 0)


def shifted(value, axis, by):
    count = lax.axis_size(axis)
    return lax.ppermute(value, axis, [(i, (i + by) % count) for i in range(count)])


def dot(a, b, contract):
    return lax.dot_general(
        a,
        b,
        (contract, ((), ())),
        precision=HIGHEST,
        preferred_element_type=jnp.float32,
    )


def inverse_factor(square):
    n = square.shape[0]
    count = n // PANEL
    sub = lax.broadcasted_iota(jnp.int32, (PANEL, n), 0)
    lane = lax.broadcasted_iota(jnp.int32, (PANEL, n), 1)

    def wide(part):
        return jnp.broadcast_to(part, (PANEL, n))

    left = [square[PANEL * i : PANEL * (i + 1), :] for i in range(count)]
    right = [jnp.where(lane == sub + PANEL * i, 1.0, 0.0) for i in range(count)]
    done = []
    for k in range(count):
        columns = [
            [wide(left[i][:, PANEL * k + j : PANEL * k + j + 1]) for i in range(k, count)]
            for j in range(PANEL)
        ]
        pivots = None
        for j in range(PANEL):
            pivot = wide(columns[j][0][j : j + 1, :])
            pivots = pivot if pivots is None else jnp.where(sub == j, pivot, pivots)
            inverse = 1.0 / pivot
            left_row = wide(left[k][j : j + 1, :])
            right_row = wide(right[k][j : j + 1, :])
            later = [wide(columns[m][0][j : j + 1, :]) for m in range(j + 1, PANEL)]
            for i in range(k, count):
                if i == k and j == PANEL - 1:
                    continue
                scale = columns[j][i - k] * inverse
                if i == k:
                    scale = jnp.where(sub > j, scale, 0.0)
                left[i] = left[i] - scale * left_row
                right[i] = right[i] - scale * right_row
                for m in range(j + 1, PANEL):
                    columns[m][i - k] = columns[m][i - k] - scale * later[m - j - 1]
        done.append(right[k] * lax.rsqrt(pivots))
    return jnp.concatenate(done, 0)


def call(kernel, name, flops, outs, *args):
    whole = pl.BlockSpec()
    smem = pl.BlockSpec(memory_space=pltpu.SMEM)
    moved = sum(math.prod(a.shape) * a.dtype.itemsize for a in (*args, *outs))
    return pl.pallas_call(
        kernel,
        out_shape=outs,
        in_specs=[smem if a.ndim == 1 else whole for a in args],
        out_specs=[whole] * len(outs),
        compiler_params=pltpu.CompilerParams(vmem_limit_bytes=VMEM_LIMIT),
        cost_estimate=pl.CostEstimate(flops=flops, bytes_accessed=moved, transcendentals=0),
        name=name,
    )(*args)


def f32(*shape):
    return jax.ShapeDtypeStruct(shape, jnp.float32)


def far(*shape):
    return pltpu.HBM(shape, jnp.float32)


def gram_kernel(parts, own, gram):
    total = jnp.sum(parts[...], 0)
    own[...] = total
    gram[...] = dot(total, total, ((0,), (0,))).reshape(gram.shape)


def tile_kernel(parts, tiles):
    total = jnp.sum(parts[...], 0)
    for i in range(tiles.shape[0]):
        tiles[i] = total


def factor_kernel(shares, out):
    gram = shares[...].reshape(out.shape)
    n = gram.shape[0] // 2
    top = inverse_factor(gram[:n, :n])
    low = dot(gram[n:, :n], top, ((1,), (1,)))
    bottom = inverse_factor(gram[n:, n:] - dot(low, low, ((1,), (1,))))
    out[:n, :n] = top
    out[:n, n:] = jnp.zeros((n, n), jnp.float32)
    out[n:, n:] = bottom
    out[n:, :n] = -dot(bottom, dot(low, top, ((1,), (0,))), ((1,), (0,)))


def place_kernel(mine, *refs):
    sketch, half = refs[-2:]
    count = len(refs) - 2
    size = refs[0].shape[0]
    for k in range(count):
        member = lax.rem(mine[0] + count - k, count)
        rows = pl.ds(pl.multiple_of(member * size, size), size)
        block = refs[k][...]
        sketch[rows, :] = block
        half[rows, :] = block.astype(half.dtype)


def solve_kernel(inverse, parts, out):
    total = jnp.sum(parts[...], 0)
    out[...] = dot(inverse[...], total, ((1,), (0,))).reshape(out.shape)


def sketch_kernel(gradients, projection, partial, held, weights, sems):
    blocks, size, _ = partial.shape
    first = pltpu.make_async_copy(projection, weights, sems.at[blocks])
    first.start()
    copies = []
    for i in range(blocks):
        part = pl.ds(i * size, size)
        copies.append(
            pltpu.make_async_copy(gradients.at[part], held.at[part], sems.at[i])
        )
        copies[-1].start()
    first.wait()
    for i in range(blocks):
        copies[i].wait()
        partial[i] = jnp.dot(
            held[i * size : (i + 1) * size, :],
            weights[...],
            preferred_element_type=jnp.float32,
        )


def sketch_blocks(gradients, projection, blocks):
    rows, feats = gradients.shape
    rank = projection.shape[1]
    return pl.pallas_call(
        sketch_kernel,
        out_shape=[
            f32(blocks, rows // blocks, rank),
            jax.ShapeDtypeStruct(gradients.shape, gradients.dtype),
        ],
        in_specs=[pl.BlockSpec(memory_space=pltpu.HBM)] * 2,
        out_specs=[pl.BlockSpec(), pl.BlockSpec(memory_space=pltpu.VMEM)],
        scratch_shapes=[
            pltpu.VMEM(projection.shape, projection.dtype),
            pltpu.SemaphoreType.DMA((blocks + 1,)),
        ],
        compiler_params=pltpu.CompilerParams(vmem_limit_bytes=VMEM_LIMIT),
        cost_estimate=pl.CostEstimate(
            flops=2 * rows * feats * rank,
            bytes_accessed=2 * feats * (rows + rank),
            transcendentals=0,
        ),
        name="sketch",
    )(
        pltpu.with_memory_space_constraint(gradients, pltpu.HBM),
        pltpu.with_memory_space_constraint(projection, pltpu.HBM),
    )


def moment_kernel(side, half, gradients, *refs):
    out = refs[-1]
    count, _, width = out.shape
    turned = half[...].T
    for i in range(count):
        columns = pl.ds(pl.multiple_of((side[0] * count + i) * width, width), width)
        value = jnp.dot(turned, gradients[:, columns], preferred_element_type=jnp.float32)
        out[i] = value if len(refs) == 1 else value + refs[0][i]


def moment_blocks(half, gradients, side, count, *added):
    rows, rank = half.shape
    width = gradients.shape[1] // (2 * count)
    vmem, whole = pl.BlockSpec(memory_space=pltpu.VMEM), pl.BlockSpec()
    return pl.pallas_call(
        moment_kernel,
        out_shape=far(count, rank, width),
        in_specs=[pl.BlockSpec(memory_space=pltpu.SMEM), whole, vmem]
        + [whole] * len(added),
        out_specs=whole,
        compiler_params=pltpu.CompilerParams(vmem_limit_bytes=VMEM_LIMIT),
        cost_estimate=pl.CostEstimate(
            flops=2 * rows * rank * width * count,
            bytes_accessed=rows * width * count * 2 + rank * width * count * 4,
            transcendentals=0,
        ),
        name="moment",
    )(side, half, gradients, *added)


def on_device(gradients, projection):
    rows, feats = gradients.shape
    rank = projection.shape[1]
    scale = float(rows * lax.axis_size(ROWS)) ** 0.5
    cores, xs = lax.axis_size("core"), lax.axis_size("x")
    core = lax.axis_index("core").astype(jnp.int32)

    near, members = lax.axis_size(NEAR), lax.axis_size(ROWS)
    zs, groups = lax.axis_size("z"), lax.axis_size("y")
    width = feats // (cores * xs)

    with jax.named_scope("sketch"):
        partial, held = sketch_blocks(gradients, projection, groups)
        parts = exchange(partial, "y")

    with jax.named_scope("gram"):
        own, shares = call(
            gram_kernel,
            "gram",
            12 * rows // groups * rank**2,
            [far(rows // groups, rank), far(near, rank // near, rank)],
            parts,
        )
        shares = exchange(shares, NEAR)

    with jax.named_scope("gram"):
        (shares,) = call(tile_kernel, "tile", SHORT, [far(zs, rank // near, rank)], shares)

    with jax.named_scope("gather"):
        others = [shifted(own, "y", k) for k in range(1, groups)]
        mine = lax.axis_index("y").astype(jnp.int32)[None]
        sketch, half = call(
            place_kernel,
            "place",
            SHORT,
            [far(rows, rank), jax.ShapeDtypeStruct((rows, rank), jnp.bfloat16)],
            mine,
            own,
            *others,
        )

    with jax.named_scope("gram"):
        shares = exchange(shares, "z")
        (shares,) = call(
            tile_kernel, "tile", SHORT, [far(near, rank // near, rank)], shares
        )
        shares = exchange(shares, NEAR)

    with jax.named_scope("factor"):
        (inverse,) = call(factor_kernel, "factor", 10**10, [f32(rank, rank)], shares)

    with jax.named_scope("moment"):
        away = moment_blocks(half, held, (1 - core)[None], xs)
        away = lax.ppermute(away, "core", [(0, 1), (1, 0)])
        moment = exchange(moment_blocks(half, held, core[None], xs, away), "x")

    with jax.named_scope("reduced"):
        (parts,) = call(
            solve_kernel,
            "solve",
            12 * rank**2 * width,
            [f32(members, rank // members, width)],
            inverse,
            moment,
        )
        parts = exchange(parts, ROWS)
        parts = parts.reshape(zs, xs, cores, rank // members, width).sum(0)
        reduced = parts.transpose(2, 1, 0, 3).reshape(rank // members, feats)

    with jax.named_scope("basis"):
        basis = dot(sketch, inverse, ((1,), (1,))) * scale
    return (basis, reduced)


def solution(mesh):
    devices = mesh.devices.reshape(16, 4, 2, 4)
    fine = Mesh(devices, ("z", "x", "core", "y"))
    in_specs = (P(ROWS, "y"), P("y", None))
    out_specs = (P(ROWS, None), P(ROWS, "y"))
    return jax.shard_map(
        on_device, mesh=fine, in_specs=in_specs, out_specs=out_specs, check_vma=False
    )
```

```python
import functools
import math

import jax
import jax.numpy as jnp
from jax import lax
from jax.experimental import pallas as pl
from jax.experimental.pallas import tpu as pltpu
from jax.sharding import Mesh
from jax.sharding import PartitionSpec as P

HIGHEST = lax.Precision.HIGHEST
ROWS = ("far", "pair", "x", "core")
DEEP = ("far", "pair")
CROSS = ("pair", "x")
NEAR = ("x", "core", "y")
GROUPS = 4
PANEL = 8
SHORT = 3 * 10**10
VMEM_LIMIT = 8 * 1024 * 1024


def exchange(blocks, axes):
    return lax.all_to_all(blocks, axes, 0, 0)


def shifted(value, axis, by):
    count = lax.axis_size(axis)
    return lax.ppermute(value, axis, [(i, (i + by) % count) for i in range(count)])


def dot(a, b, contract):
    return lax.dot_general(
        a,
        b,
        (contract, ((), ())),
        precision=HIGHEST,
        preferred_element_type=jnp.float32,
    )


def inverse_factor(square):
    n = square.shape[0]
    count = n // PANEL
    sub = lax.broadcasted_iota(jnp.int32, (PANEL, n), 0)
    lane = lax.broadcasted_iota(jnp.int32, (PANEL, n), 1)

    def wide(part):
        return jnp.broadcast_to(part, (PANEL, n))

    left = [square[PANEL * i : PANEL * (i + 1), :] for i in range(count)]
    right = [jnp.where(lane == sub + PANEL * i, 1.0, 0.0) for i in range(count)]
    done = []
    for k in range(count):
        columns = [
            [wide(left[i][:, PANEL * k + j : PANEL * k + j + 1]) for i in range(k, count)]
            for j in range(PANEL)
        ]
        pivots = None
        for j in range(PANEL):
            pivot = wide(columns[j][0][j : j + 1, :])
            pivots = pivot if pivots is None else jnp.where(sub == j, pivot, pivots)
            inverse = 1.0 / pivot
            left_row = wide(left[k][j : j + 1, :])
            right_row = wide(right[k][j : j + 1, :])
            later = [wide(columns[m][0][j : j + 1, :]) for m in range(j + 1, PANEL)]
            for i in range(k, count):
                if i == k and j == PANEL - 1:
                    continue
                scale = columns[j][i - k] * inverse
                if i == k:
                    scale = jnp.where(sub > j, scale, 0.0)
                left[i] = left[i] - scale * left_row
                right[i] = right[i] - scale * right_row
                for m in range(j + 1, PANEL):
                    columns[m][i - k] = columns[m][i - k] - scale * later[m - j - 1]
        done.append(right[k] * lax.rsqrt(pivots))
    return jnp.concatenate(done, 0)


def call(kernel, name, flops, outs, *args):
    whole = pl.BlockSpec()
    smem = pl.BlockSpec(memory_space=pltpu.SMEM)
    moved = sum(math.prod(a.shape) * a.dtype.itemsize for a in (*args, *outs))
    return pl.pallas_call(
        kernel,
        out_shape=outs,
        in_specs=[smem if a.ndim == 1 else whole for a in args],
        out_specs=[whole] * len(outs),
        compiler_params=pltpu.CompilerParams(vmem_limit_bytes=VMEM_LIMIT),
        cost_estimate=pl.CostEstimate(flops=flops, bytes_accessed=moved, transcendentals=0),
        name=name,
    )(*args)


def f32(*shape):
    return jax.ShapeDtypeStruct(shape, jnp.float32)


def far(*shape):
    return pltpu.HBM(shape, jnp.float32)


def gram_kernel(parts, own, gram):
    total = jnp.sum(parts[...], 0)
    own[...] = total
    gram[...] = dot(total, total, ((0,), (0,))).reshape(gram.shape)


def tile_kernel(parts, tiles):
    total = jnp.sum(parts[...], 0)
    for i in range(tiles.shape[0]):
        tiles[i] = total


def factor_kernel(shares, out):
    gram = shares[...].reshape(out.shape)
    n = gram.shape[0] // 2
    top = inverse_factor(gram[:n, :n])
    low = dot(gram[n:, :n], top, ((1,), (1,)))
    bottom = inverse_factor(gram[n:, n:] - dot(low, low, ((1,), (1,))))
    out[:n, :n] = top
    out[:n, n:] = jnp.zeros((n, n), jnp.float32)
    out[n:, n:] = bottom
    out[n:, :n] = -dot(bottom, dot(low, top, ((1,), (0,))), ((1,), (0,)))


def members(place, refs):
    count = len(refs)
    size = refs[0].shape[0]
    for k, ref in enumerate(refs):
        member = lax.rem(place + count - k, count)
        yield pl.ds(pl.multiple_of(member * size, size), size), ref


def basis_kernel(scale, place, inverse, *refs):
    blocks, out = refs[:-1], refs[-1]
    for rows, block in members(place[0], blocks):
        out[rows, :] = dot(block[...], inverse[...], ((1,), (1,))) * scale


def solve_kernel(inverse, parts, out):
    total = jnp.sum(parts[...], 0)
    out[...] = dot(inverse[...], total, ((1,), (0,))).reshape(out.shape)


def sketch_kernel(gradients, projection, partial, held, weights, sems):
    blocks, size, _ = partial.shape
    first = pltpu.make_async_copy(projection, weights, sems.at[blocks])
    first.start()
    copies = []
    for i in range(blocks):
        part = pl.ds(i * size, size)
        copies.append(
            pltpu.make_async_copy(gradients.at[part], held.at[part], sems.at[i])
        )
        copies[-1].start()
    first.wait()
    for i in range(blocks):
        copies[i].wait()
        partial[i] = jnp.dot(
            held[i * size : (i + 1) * size, :],
            weights[...],
            preferred_element_type=jnp.float32,
        )


def sketch_blocks(gradients, projection, blocks):
    rows, feats = gradients.shape
    rank = projection.shape[1]
    return pl.pallas_call(
        sketch_kernel,
        out_shape=[
            f32(blocks, rows // blocks, rank),
            jax.ShapeDtypeStruct(gradients.shape, gradients.dtype),
        ],
        in_specs=[pl.BlockSpec(memory_space=pltpu.HBM)] * 2,
        out_specs=[pl.BlockSpec(), pl.BlockSpec(memory_space=pltpu.VMEM)],
        scratch_shapes=[
            pltpu.VMEM(projection.shape, projection.dtype),
            pltpu.SemaphoreType.DMA((blocks + 1,)),
        ],
        compiler_params=pltpu.CompilerParams(vmem_limit_bytes=VMEM_LIMIT),
        cost_estimate=pl.CostEstimate(
            flops=2 * rows * feats * rank,
            bytes_accessed=2 * feats * (rows + rank),
            transcendentals=0,
        ),
        name="sketch",
    )(
        pltpu.with_memory_space_constraint(gradients, pltpu.HBM),
        pltpu.with_memory_space_constraint(projection, pltpu.HBM),
    )


def moment_kernel(place, gradients, *refs):
    half, out = refs[-1], refs[-2]
    blocks, added = refs[:GROUPS], refs[GROUPS:-2]
    for rows, block in members(place[1], blocks):
        half[rows, :] = block[...].astype(half.dtype)
    turned = half[...].T
    count, _, width = out.shape
    for i in range(0, count, 2):
        start = pl.multiple_of((place[0] * count + i) * width, 2 * width)
        value = jnp.dot(
            turned,
            gradients[:, pl.ds(start, 2 * width)],
            preferred_element_type=jnp.float32,
        )
        for j in range(2):
            part = value[:, j * width : (j + 1) * width]
            out[i + j] = part + added[0][i + j] if added else part


def moment_blocks(place, gradients, blocks, count, flops, *added):
    rows, feats = gradients.shape
    rank = blocks[0].shape[1]
    width = feats // (2 * count)
    whole = pl.BlockSpec()
    return pl.pallas_call(
        moment_kernel,
        out_shape=far(count, rank, width),
        in_specs=[
            pl.BlockSpec(memory_space=pltpu.SMEM),
            pl.BlockSpec(memory_space=pltpu.VMEM),
        ]
        + [whole] * (len(blocks) + len(added)),
        out_specs=whole,
        scratch_shapes=[pltpu.VMEM((rows, rank), jnp.bfloat16)],
        compiler_params=pltpu.CompilerParams(vmem_limit_bytes=VMEM_LIMIT),
        cost_estimate=pl.CostEstimate(
            flops=flops,
            bytes_accessed=rows * width * count * 2 + rank * width * count * 4,
            transcendentals=0,
        ),
        name="moment",
    )(place, gradients, *blocks, *added)


def on_device(gradients, projection):
    rows, feats = gradients.shape
    rank = projection.shape[1]
    members_of_rows, near = lax.axis_size(ROWS), lax.axis_size(NEAR)
    deep, pairs, xs, cores = (lax.axis_size(a) for a in (DEEP, "pair", "x", "core"))
    scale = float(rows * members_of_rows) ** 0.5
    core = lax.axis_index("core").astype(jnp.int32)
    mine = lax.axis_index("y").astype(jnp.int32)
    size = rank // near
    width = feats // (cores * pairs * xs)

    with jax.named_scope("sketch"):
        partial, held = sketch_blocks(gradients, projection, GROUPS)
        parts = exchange(partial, "y")

    with jax.named_scope("gram"):
        own, shares = call(
            gram_kernel,
            "gram",
            12 * rows // GROUPS * rank**2,
            [far(rows // GROUPS, rank), far(near, size, rank)],
            parts,
        )
        shares = exchange(shares, NEAR)
        (shares,) = call(tile_kernel, "tile", SHORT, [far(deep, size, rank)], shares)
        shares = exchange(shares, DEEP)
        (shares,) = call(tile_kernel, "tile", SHORT, [far(near, size, rank)], shares)
        shares = exchange(shares, NEAR)

    with jax.named_scope("factor"):
        (inverse,) = call(factor_kernel, "factor", 10**10, [f32(rank, rank)], shares)

    with jax.named_scope("gather"):
        blocks = [own] + [shifted(own, "y", k) for k in range(1, GROUPS)]
        blocks = [pltpu.with_memory_space_constraint(b, pltpu.HBM) for b in blocks]

    with jax.named_scope("moment"):
        count = pairs * xs
        away = moment_blocks(jnp.stack([1 - core, mine]), held, blocks, count, SHORT)
        away = lax.ppermute(away, "core", [(0, 1), (1, 0)])
        moment = moment_blocks(
            jnp.stack([core, mine]), held, blocks, count, 10**9, away
        )
        moment = exchange(moment, CROSS)

    with jax.named_scope("reduced"):
        (parts,) = call(
            solve_kernel,
            "solve",
            12 * rank**2 * width,
            [f32(members_of_rows, rank // members_of_rows, width)],
            inverse,
            moment,
        )
        parts = exchange(parts, ROWS)
        parts = parts.reshape(-1, pairs, xs, cores, rank // members_of_rows, width).sum(0)
        reduced = parts.transpose(3, 2, 0, 1, 4).reshape(rank // members_of_rows, feats)

    with jax.named_scope("basis"):
        (basis,) = call(
            functools.partial(basis_kernel, scale),
            "basis",
            12 * rows * rank**2,
            [f32(rows, rank)],
            mine[None],
            inverse,
            *blocks,
        )
    return (basis, reduced)


def solution(mesh):
    devices = mesh.devices.reshape(8, 2, 4, 2, 4)
    fine = Mesh(devices, ("far", "pair", "x", "core", "y"))
    in_specs = (P(ROWS, "y"), P("y", None))
    out_specs = (P(ROWS, None), P(ROWS, "y"))
    return jax.shard_map(
        on_device, mesh=fine, in_specs=in_specs, out_specs=out_specs, check_vma=False
    )
```

```python
import functools
import math

import jax
import jax.numpy as jnp
from jax import lax
from jax.experimental import pallas as pl
from jax.experimental.pallas import tpu as pltpu
from jax.sharding import Mesh
from jax.sharding import PartitionSpec as P

HIGHEST = lax.Precision.HIGHEST
ROWS = ("far", "pair", "x", "core")
DEEP = ("far", "pair")
NEAR = ("x", "core", "y")
GROUPS = 4
PANEL = 8
SHORT = 3 * 10**10
VMEM_LIMIT = 8 * 1024 * 1024


def exchange(blocks, axes):
    return lax.all_to_all(blocks, axes, 0, 0)


def shifted(value, axis, by):
    count = lax.axis_size(axis)
    return lax.ppermute(value, axis, [(i, (i + by) % count) for i in range(count)])


def dot(a, b, contract):
    return lax.dot_general(
        a,
        b,
        (contract, ((), ())),
        precision=HIGHEST,
        preferred_element_type=jnp.float32,
    )


def inverse_factor(square):
    n = square.shape[0]
    count = n // PANEL
    sub = lax.broadcasted_iota(jnp.int32, (PANEL, n), 0)
    lane = lax.broadcasted_iota(jnp.int32, (PANEL, n), 1)

    def wide(part):
        return jnp.broadcast_to(part, (PANEL, n))

    left = [square[PANEL * i : PANEL * (i + 1), :] for i in range(count)]
    right = [jnp.where(lane == sub + PANEL * i, 1.0, 0.0) for i in range(count)]
    done = []
    for k in range(count):
        columns = [
            [wide(left[i][:, PANEL * k + j : PANEL * k + j + 1]) for i in range(k, count)]
            for j in range(PANEL)
        ]
        pivots = None
        for j in range(PANEL):
            pivot = wide(columns[j][0][j : j + 1, :])
            pivots = pivot if pivots is None else jnp.where(sub == j, pivot, pivots)
            inverse = 1.0 / pivot
            left_row = wide(left[k][j : j + 1, :])
            right_row = wide(right[k][j : j + 1, :])
            later = [wide(columns[m][0][j : j + 1, :]) for m in range(j + 1, PANEL)]
            for i in range(k, count):
                if i == k and j == PANEL - 1:
                    continue
                scale = columns[j][i - k] * inverse
                if i == k:
                    scale = jnp.where(sub > j, scale, 0.0)
                left[i] = left[i] - scale * left_row
                right[i] = right[i] - scale * right_row
                for m in range(j + 1, PANEL):
                    columns[m][i - k] = columns[m][i - k] - scale * later[m - j - 1]
        done.append(right[k] * lax.rsqrt(pivots))
    return jnp.concatenate(done, 0)


def call(kernel, name, flops, outs, *args):
    whole = pl.BlockSpec()
    smem = pl.BlockSpec(memory_space=pltpu.SMEM)
    moved = sum(math.prod(a.shape) * a.dtype.itemsize for a in (*args, *outs))
    return pl.pallas_call(
        kernel,
        out_shape=outs,
        in_specs=[smem if a.ndim == 1 else whole for a in args],
        out_specs=[whole] * len(outs),
        compiler_params=pltpu.CompilerParams(vmem_limit_bytes=VMEM_LIMIT),
        cost_estimate=pl.CostEstimate(flops=flops, bytes_accessed=moved, transcendentals=0),
        name=name,
    )(*args)


def f32(*shape):
    return jax.ShapeDtypeStruct(shape, jnp.float32)


def far(*shape):
    return pltpu.HBM(shape, jnp.float32)


def gram_kernel(parts, own, gram):
    total = jnp.sum(parts[...], 0)
    own[...] = total
    gram[...] = dot(total, total, ((0,), (0,))).reshape(gram.shape)


def tile_kernel(parts, tiles):
    total = jnp.sum(parts[...], 0)
    for i in range(tiles.shape[0]):
        tiles[i] = total


def factor_kernel(shares, out):
    gram = shares[...].reshape(out.shape)
    n = gram.shape[0] // 2
    top = inverse_factor(gram[:n, :n])
    low = dot(gram[n:, :n], top, ((1,), (1,)))
    bottom = inverse_factor(gram[n:, n:] - dot(low, low, ((1,), (1,))))
    out[:n, :n] = top
    out[:n, n:] = jnp.zeros((n, n), jnp.float32)
    out[n:, n:] = bottom
    out[n:, :n] = -dot(bottom, dot(low, top, ((1,), (0,))), ((1,), (0,)))


def members(place, refs):
    count = len(refs)
    size = refs[0].shape[0]
    for k, ref in enumerate(refs):
        member = lax.rem(place + count - k, count)
        yield pl.ds(pl.multiple_of(member * size, size), size), ref


def basis_kernel(scale, place, inverse, *refs):
    blocks, out = refs[:-1], refs[-1]
    for rows, block in members(place[0], blocks):
        out[rows, :] = dot(block[...], inverse[...], ((1,), (1,))) * scale


def solve_kernel(inverse, parts, out):
    total = jnp.sum(parts[...], 0)
    out[...] = dot(inverse[...], total, ((1,), (0,))).reshape(out.shape)


def sketch_kernel(gradients, projection, partial, held, weights, sems):
    blocks, size, _ = partial.shape
    first = pltpu.make_async_copy(projection, weights, sems.at[blocks])
    first.start()
    copies = []
    for i in range(blocks):
        part = pl.ds(i * size, size)
        copies.append(
            pltpu.make_async_copy(gradients.at[part], held.at[part], sems.at[i])
        )
        copies[-1].start()
    first.wait()
    for i in range(blocks):
        copies[i].wait()
        partial[i] = jnp.dot(
            held[i * size : (i + 1) * size, :],
            weights[...],
            preferred_element_type=jnp.float32,
        )


def sketch_blocks(gradients, projection, blocks):
    rows, feats = gradients.shape
    rank = projection.shape[1]
    return pl.pallas_call(
        sketch_kernel,
        out_shape=[
            f32(blocks, rows // blocks, rank),
            jax.ShapeDtypeStruct(gradients.shape, gradients.dtype),
        ],
        in_specs=[pl.BlockSpec(memory_space=pltpu.HBM)] * 2,
        out_specs=[pl.BlockSpec(), pl.BlockSpec(memory_space=pltpu.VMEM)],
        scratch_shapes=[
            pltpu.VMEM(projection.shape, projection.dtype),
            pltpu.SemaphoreType.DMA((blocks + 1,)),
        ],
        compiler_params=pltpu.CompilerParams(vmem_limit_bytes=VMEM_LIMIT),
        cost_estimate=pl.CostEstimate(
            flops=2 * rows * feats * rank,
            bytes_accessed=2 * feats * (rows + rank),
            transcendentals=0,
        ),
        name="sketch",
    )(
        pltpu.with_memory_space_constraint(gradients, pltpu.HBM),
        pltpu.with_memory_space_constraint(projection, pltpu.HBM),
    )


def moment_kernel(place, gradients, *refs):
    blocks, added = refs[:GROUPS], refs[GROUPS]
    outs, half = refs[GROUPS:-1], refs[-1]
    for rows, block in members(place[1], blocks):
        half[rows, :] = block[...].astype(half.dtype)
    turned = half[...].T
    single = len(outs) == 1
    outs = outs if single else outs[1:]
    count, _, width = outs[0].shape
    total = count * len(outs)
    for n, out in enumerate(outs):
        for i in range(0, count, 2):
            block = i if single else lax.rem(place[2] + n, 2) * count + i
            start = pl.multiple_of((place[0] * total + block) * width, 2 * width)
            value = jnp.dot(
                turned,
                gradients[:, pl.ds(start, 2 * width)],
                preferred_element_type=jnp.float32,
            )
            for j in range(2):
                part = value[:, j * width : (j + 1) * width]
                out[i + j] = part if single else part + added[block + j]


def moment_blocks(place, gradients, blocks, count, flops, *added):
    rows, feats = gradients.shape
    rank = blocks[0].shape[1]
    width = feats // (2 * count)
    whole = pl.BlockSpec()
    outs = [far(count // 2, rank, width)] * 2 if added else far(count, rank, width)
    return pl.pallas_call(
        moment_kernel,
        out_shape=outs,
        in_specs=[
            pl.BlockSpec(memory_space=pltpu.SMEM),
            pl.BlockSpec(memory_space=pltpu.VMEM),
        ]
        + [whole] * (len(blocks) + len(added)),
        out_specs=[whole] * 2 if added else whole,
        scratch_shapes=[pltpu.VMEM((rows, rank), jnp.bfloat16)],
        compiler_params=pltpu.CompilerParams(vmem_limit_bytes=VMEM_LIMIT),
        cost_estimate=pl.CostEstimate(
            flops=flops,
            bytes_accessed=rows * width * count * 2 + rank * width * count * 4,
            transcendentals=0,
        ),
        name="moment",
    )(place, gradients, *blocks, *added)


def add_kernel(a, b, out):
    out[...] = a[...] + b[...]


def on_device(gradients, projection):
    rows, feats = gradients.shape
    rank = projection.shape[1]
    members_of_rows, near = lax.axis_size(ROWS), lax.axis_size(NEAR)
    deep, pairs, xs, cores = (lax.axis_size(a) for a in (DEEP, "pair", "x", "core"))
    scale = float(rows * members_of_rows) ** 0.5
    core = lax.axis_index("core").astype(jnp.int32)
    mine = lax.axis_index("y").astype(jnp.int32)
    size = rank // near
    width = feats // (cores * pairs * xs)

    with jax.named_scope("sketch"):
        partial, held = sketch_blocks(gradients, projection, GROUPS)
        parts = exchange(partial, "y")

    with jax.named_scope("gram"):
        own, shares = call(
            gram_kernel,
            "gram",
            12 * rows // GROUPS * rank**2,
            [far(rows // GROUPS, rank), far(near, size, rank)],
            parts,
        )
        shares = exchange(shares, NEAR)
        (shares,) = call(tile_kernel, "tile", SHORT, [far(deep, size, rank)], shares)
        shares = exchange(shares, DEEP)
        (shares,) = call(tile_kernel, "tile", SHORT, [far(near, size, rank)], shares)
        shares = exchange(shares, NEAR)

    with jax.named_scope("factor"):
        (inverse,) = call(factor_kernel, "factor", 10**10, [f32(rank, rank)], shares)

    with jax.named_scope("gather"):
        blocks = [own] + [shifted(own, "y", k) for k in range(1, GROUPS)]
        blocks = [pltpu.with_memory_space_constraint(b, pltpu.HBM) for b in blocks]

    with jax.named_scope("moment"):
        swap = [(0, 1), (1, 0)]
        pair = lax.axis_index("pair").astype(jnp.int32)
        count = pairs * xs
        away = moment_blocks(jnp.stack([1 - core, mine]), held, blocks, count, SHORT)
        away = lax.ppermute(away, "core", swap)
        kept, given = moment_blocks(
            jnp.stack([core, mine, pair]), held, blocks, count, 10**8, away
        )
        given = lax.ppermute(given, "pair", swap)
        (moment,) = call(add_kernel, "add", 0, [far(xs, rank, width)], kept, given)
        moment = exchange(moment, "x")

    with jax.named_scope("reduced"):
        (parts,) = call(
            solve_kernel,
            "solve",
            12 * rank**2 * width,
            [f32(members_of_rows, rank // members_of_rows, width)],
            inverse,
            moment,
        )
        parts = exchange(parts, ROWS)
        parts = parts.reshape(-1, pairs, xs, cores, rank // members_of_rows, width).sum(0)
        reduced = parts.transpose(3, 2, 0, 1, 4).reshape(rank // members_of_rows, feats)

    with jax.named_scope("basis"):
        (basis,) = call(
            functools.partial(basis_kernel, scale),
            "basis",
            12 * rows * rank**2,
            [f32(rows, rank)],
            mine[None],
            inverse,
            *blocks,
        )
    return (basis, reduced)


def solution(mesh):
    devices = mesh.devices.reshape(8, 2, 4, 2, 4)
    fine = Mesh(devices, ("far", "pair", "x", "core", "y"))
    in_specs = (P(ROWS, "y"), P("y", None))
    out_specs = (P(ROWS, None), P(ROWS, "y"))
    return jax.shard_map(
        on_device, mesh=fine, in_specs=in_specs, out_specs=out_specs, check_vma=False
    )
```

```python
import functools
import math

import jax
import jax.numpy as jnp
from jax import lax
from jax.experimental import pallas as pl
from jax.experimental.pallas import tpu as pltpu
from jax.sharding import Mesh
from jax.sharding import PartitionSpec as P

HIGHEST = lax.Precision.HIGHEST
ROWS = ("far", "pair", "x", "core")
DEEP = ("far", "pair")
CROSS = ("pair", "x")
NEAR = ("x", "core", "y")
GROUPS = 4
PIECES = 4
PANEL = 8
SHORT = 3 * 10**10
VMEM_LIMIT = 8 * 1024 * 1024


def exchange(blocks, axes):
    return lax.all_to_all(blocks, axes, 0, 0)


def shifted(value, axis, by):
    count = lax.axis_size(axis)
    return lax.ppermute(value, axis, [(i, (i + by) % count) for i in range(count)])


def dot(a, b, contract):
    return lax.dot_general(
        a,
        b,
        (contract, ((), ())),
        precision=HIGHEST,
        preferred_element_type=jnp.float32,
    )


def inverse_factor(square):
    n = square.shape[0]
    count = n // PANEL
    sub = lax.broadcasted_iota(jnp.int32, (PANEL, n), 0)
    lane = lax.broadcasted_iota(jnp.int32, (PANEL, n), 1)

    def wide(part):
        return jnp.broadcast_to(part, (PANEL, n))

    left = [square[PANEL * i : PANEL * (i + 1), :] for i in range(count)]
    right = [jnp.where(lane == sub + PANEL * i, 1.0, 0.0) for i in range(count)]
    done = []
    for k in range(count):
        columns = [
            [wide(left[i][:, PANEL * k + j : PANEL * k + j + 1]) for i in range(k, count)]
            for j in range(PANEL)
        ]
        pivots = None
        for j in range(PANEL):
            pivot = wide(columns[j][0][j : j + 1, :])
            pivots = pivot if pivots is None else jnp.where(sub == j, pivot, pivots)
            inverse = 1.0 / pivot
            left_row = wide(left[k][j : j + 1, :])
            right_row = wide(right[k][j : j + 1, :])
            later = [wide(columns[m][0][j : j + 1, :]) for m in range(j + 1, PANEL)]
            for i in range(k, count):
                if i == k and j == PANEL - 1:
                    continue
                scale = columns[j][i - k] * inverse
                if i == k:
                    scale = jnp.where(sub > j, scale, 0.0)
                left[i] = left[i] - scale * left_row
                right[i] = right[i] - scale * right_row
                for m in range(j + 1, PANEL):
                    columns[m][i - k] = columns[m][i - k] - scale * later[m - j - 1]
        done.append(right[k] * lax.rsqrt(pivots))
    return jnp.concatenate(done, 0)


def call(kernel, name, flops, outs, *args, scratch=()):
    whole = pl.BlockSpec()
    smem = pl.BlockSpec(memory_space=pltpu.SMEM)
    moved = sum(math.prod(a.shape) * a.dtype.itemsize for a in (*args, *outs))
    return pl.pallas_call(
        kernel,
        out_shape=outs,
        in_specs=[smem if a.ndim == 1 else whole for a in args],
        out_specs=[whole] * len(outs),
        scratch_shapes=scratch,
        compiler_params=pltpu.CompilerParams(vmem_limit_bytes=VMEM_LIMIT),
        cost_estimate=pl.CostEstimate(flops=flops, bytes_accessed=moved, transcendentals=0),
        name=name,
    )(*args)


def f32(*shape):
    return jax.ShapeDtypeStruct(shape, jnp.float32)


def far(*shape):
    return pltpu.HBM(shape, jnp.float32)


def gram_kernel(parts, own, gram):
    total = jnp.sum(parts[...], 0)
    own[...] = total
    n = total.shape[1] // 2
    left = dot(total, total[:, :n], ((0,), (0,)))
    right = dot(total[:, n:], total[:, n:], ((0,), (0,)))
    packed = jnp.concatenate([left[:n], left[n:], right], 1)
    gram[...] = packed.reshape(gram.shape)


def tile_kernel(parts, tiles):
    total = jnp.sum(parts[...], 0)
    for i in range(tiles.shape[0]):
        tiles[i] = total


def factor_kernel(shares, out, packed):
    n = out.shape[0] // 2
    packed[...] = shares[...].reshape(packed.shape)
    top = inverse_factor(packed[:, :n])
    low = dot(packed[:, n : 2 * n], top, ((1,), (1,)))
    bottom = inverse_factor(packed[:, 2 * n :] - dot(low, low, ((1,), (1,))))
    out[:n, :n] = top
    out[:n, n:] = jnp.zeros((n, n), jnp.float32)
    out[n:, n:] = bottom
    out[n:, :n] = -dot(bottom, dot(low, top, ((1,), (0,))), ((1,), (0,)))


def members(place, refs):
    count = len(refs)
    size = refs[0].shape[0]
    for k, ref in enumerate(refs):
        member = lax.rem(place + count - k, count)
        yield pl.ds(pl.multiple_of(member * size, size), size), ref


def basis_kernel(scale, place, inverse, *refs):
    blocks, out = refs[:-1], refs[-1]
    for rows, block in members(place[0], blocks):
        out[rows, :] = dot(block[...], inverse[...], ((1,), (1,))) * scale


def solve_kernel(inverse, parts, out):
    total = jnp.sum(parts[...], 0)
    out[...] = dot(inverse[...], total, ((1,), (0,))).reshape(out.shape)


def sketch_kernel(gradients, projection, partial, held, weights, sems):
    copies = [pltpu.make_async_copy(projection, weights, sems.at[0])]
    size = held.shape[0] // PIECES
    for i in range(PIECES):
        part = pl.ds(i * size, size)
        copies.append(
            pltpu.make_async_copy(gradients.at[part], held.at[part], sems.at[i + 1])
        )
    for copy in copies:
        copy.start()
    for copy in copies:
        copy.wait()
    value = jnp.dot(held[...], weights[...], preferred_element_type=jnp.float32)
    partial[...] = value.reshape(partial.shape)


def sketch_blocks(gradients, projection, blocks):
    rows, feats = gradients.shape
    rank = projection.shape[1]
    return pl.pallas_call(
        sketch_kernel,
        out_shape=[
            f32(blocks, rows // blocks, rank),
            jax.ShapeDtypeStruct(gradients.shape, gradients.dtype),
        ],
        in_specs=[pl.BlockSpec(memory_space=pltpu.HBM)] * 2,
        out_specs=[pl.BlockSpec(), pl.BlockSpec(memory_space=pltpu.VMEM)],
        scratch_shapes=[
            pltpu.VMEM(projection.shape, projection.dtype),
            pltpu.SemaphoreType.DMA((PIECES + 1,)),
        ],
        compiler_params=pltpu.CompilerParams(vmem_limit_bytes=VMEM_LIMIT),
        cost_estimate=pl.CostEstimate(
            flops=2 * rows * feats * rank,
            bytes_accessed=2 * feats * (rows + rank),
            transcendentals=0,
        ),
        name="sketch",
    )(
        pltpu.with_memory_space_constraint(gradients, pltpu.HBM),
        pltpu.with_memory_space_constraint(projection, pltpu.HBM),
    )


def moment_kernel(place, gradients, *refs):
    half, out = refs[-1], refs[-2]
    blocks, added = refs[:GROUPS], refs[GROUPS:-2]
    for rows, block in members(place[1], blocks):
        half[rows, :] = block[...].astype(half.dtype)
    turned = half[...].T
    count, _, width = out.shape
    for i in range(0, count, 2):
        start = pl.multiple_of((place[0] * count + i) * width, 2 * width)
        value = jnp.dot(
            turned,
            gradients[:, pl.ds(start, 2 * width)],
            preferred_element_type=jnp.float32,
        )
        for j in range(2):
            part = value[:, j * width : (j + 1) * width]
            out[i + j] = part + added[0][i + j] if added else part


def moment_blocks(place, gradients, blocks, count, flops, *added):
    rows, feats = gradients.shape
    rank = blocks[0].shape[1]
    width = feats // (2 * count)
    whole = pl.BlockSpec()
    return pl.pallas_call(
        moment_kernel,
        out_shape=far(count, rank, width),
        in_specs=[
            pl.BlockSpec(memory_space=pltpu.SMEM),
            pl.BlockSpec(memory_space=pltpu.VMEM),
        ]
        + [whole] * (len(blocks) + len(added)),
        out_specs=whole,
        scratch_shapes=[pltpu.VMEM((rows, rank), jnp.bfloat16)],
        compiler_params=pltpu.CompilerParams(vmem_limit_bytes=VMEM_LIMIT),
        cost_estimate=pl.CostEstimate(
            flops=flops,
            bytes_accessed=rows * width * count * 2 + rank * width * count * 4,
            transcendentals=0,
        ),
        name="moment",
    )(place, gradients, *blocks, *added)


def on_device(gradients, projection):
    rows, feats = gradients.shape
    rank = projection.shape[1]
    members_of_rows, near = lax.axis_size(ROWS), lax.axis_size(NEAR)
    deep, pairs, xs, cores = (lax.axis_size(a) for a in (DEEP, "pair", "x", "core"))
    scale = float(rows * members_of_rows) ** 0.5
    core = lax.axis_index("core").astype(jnp.int32)
    mine = lax.axis_index("y").astype(jnp.int32)
    share = (rank // 2 // near, 3 * rank // 2)
    width = feats // (cores * pairs * xs)

    with jax.named_scope("sketch"):
        partial, held = sketch_blocks(gradients, projection, GROUPS)
        parts = exchange(partial, "y")

    with jax.named_scope("gram"):
        own, shares = call(
            gram_kernel,
            "gram",
            12 * rows // GROUPS * rank**2,
            [far(rows // GROUPS, rank), far(near, *share)],
            parts,
        )
        shares = exchange(shares, NEAR)
        (shares,) = call(tile_kernel, "tile", SHORT, [far(deep, *share)], shares)
        shares = exchange(shares, DEEP)
        (shares,) = call(tile_kernel, "tile", SHORT, [far(near, *share)], shares)
        shares = exchange(shares, NEAR)

    with jax.named_scope("factor"):
        (inverse,) = call(
            factor_kernel,
            "factor",
            10**10,
            [f32(rank, rank)],
            shares,
            scratch=[pltpu.VMEM((rank // 2, 3 * rank // 2), jnp.float32)],
        )

    with jax.named_scope("gather"):
        blocks = [own] + [shifted(own, "y", k) for k in range(1, GROUPS)]
        blocks = [pltpu.with_memory_space_constraint(b, pltpu.HBM) for b in blocks]

    with jax.named_scope("moment"):
        count = pairs * xs
        away = moment_blocks(jnp.stack([1 - core, mine]), held, blocks, count, SHORT)
        away = lax.ppermute(away, "core", [(0, 1), (1, 0)])
        moment = moment_blocks(
            jnp.stack([core, mine]), held, blocks, count, 10**9, away
        )
        moment = exchange(moment, CROSS)

    with jax.named_scope("reduced"):
        (parts,) = call(
            solve_kernel,
            "solve",
            12 * rank**2 * width,
            [f32(members_of_rows, rank // members_of_rows, width)],
            inverse,
            moment,
        )
        parts = exchange(parts, ROWS)
        parts = parts.reshape(-1, pairs, xs, cores, rank // members_of_rows, width).sum(0)
        reduced = parts.transpose(3, 2, 0, 1, 4).reshape(rank // members_of_rows, feats)

    with jax.named_scope("basis"):
        (basis,) = call(
            functools.partial(basis_kernel, scale),
            "basis",
            12 * rows * rank**2,
            [f32(rows, rank)],
            mine[None],
            inverse,
            *blocks,
        )
    return (basis, reduced)


def solution(mesh):
    devices = mesh.devices.reshape(8, 2, 4, 2, 4)
    fine = Mesh(devices, ("far", "pair", "x", "core", "y"))
    in_specs = (P(ROWS, "y"), P("y", None))
    out_specs = (P(ROWS, None), P(ROWS, "y"))
    return jax.shard_map(
        on_device, mesh=fine, in_specs=in_specs, out_specs=out_specs, check_vma=False
    )
```

```python
import functools
import math

import jax
import jax.numpy as jnp
from jax import lax
from jax.experimental import pallas as pl
from jax.experimental.pallas import tpu as pltpu
from jax.sharding import Mesh
from jax.sharding import PartitionSpec as P

HIGHEST = lax.Precision.HIGHEST
ROWS = ("far", "pair", "x", "core")
DEEP = ("far", "pair")
NEAR = ("x", "core", "y")
GROUPS = 4
PIECES = 4
PANEL = 8
SHORT = 3 * 10**10
VMEM_LIMIT = 8 * 1024 * 1024


def exchange(blocks, axes):
    return lax.all_to_all(blocks, axes, 0, 0)


def shifted(value, axis, by):
    count = lax.axis_size(axis)
    return lax.ppermute(value, axis, [(i, (i + by) % count) for i in range(count)])


def dot(a, b, contract):
    return lax.dot_general(
        a,
        b,
        (contract, ((), ())),
        precision=HIGHEST,
        preferred_element_type=jnp.float32,
    )


def inverse_factor(square):
    n = square.shape[0]
    count = n // PANEL
    sub = lax.broadcasted_iota(jnp.int32, (PANEL, n), 0)
    lane = lax.broadcasted_iota(jnp.int32, (PANEL, n), 1)

    def wide(part):
        return jnp.broadcast_to(part, (PANEL, n))

    left = [square[PANEL * i : PANEL * (i + 1), :] for i in range(count)]
    right = [jnp.where(lane == sub + PANEL * i, 1.0, 0.0) for i in range(count)]
    done = []
    for k in range(count):
        columns = [
            [wide(left[i][:, PANEL * k + j : PANEL * k + j + 1]) for i in range(k, count)]
            for j in range(PANEL)
        ]
        pivots = None
        for j in range(PANEL):
            pivot = wide(columns[j][0][j : j + 1, :])
            pivots = pivot if pivots is None else jnp.where(sub == j, pivot, pivots)
            inverse = 1.0 / pivot
            left_row = wide(left[k][j : j + 1, :])
            right_row = wide(right[k][j : j + 1, :])
            later = [wide(columns[m][0][j : j + 1, :]) for m in range(j + 1, PANEL)]
            for i in range(k, count):
                if i == k and j == PANEL - 1:
                    continue
                scale = columns[j][i - k] * inverse
                if i == k:
                    scale = jnp.where(sub > j, scale, 0.0)
                left[i] = left[i] - scale * left_row
                right[i] = right[i] - scale * right_row
                for m in range(j + 1, PANEL):
                    columns[m][i - k] = columns[m][i - k] - scale * later[m - j - 1]
        done.append(right[k] * lax.rsqrt(pivots))
    return jnp.concatenate(done, 0)


def call(kernel, name, flops, outs, *args, scratch=()):
    whole = pl.BlockSpec()
    smem = pl.BlockSpec(memory_space=pltpu.SMEM)
    moved = sum(math.prod(a.shape) * a.dtype.itemsize for a in (*args, *outs))
    return pl.pallas_call(
        kernel,
        out_shape=outs,
        in_specs=[smem if a.ndim == 1 else whole for a in args],
        out_specs=[whole] * len(outs),
        scratch_shapes=scratch,
        compiler_params=pltpu.CompilerParams(vmem_limit_bytes=VMEM_LIMIT),
        cost_estimate=pl.CostEstimate(flops=flops, bytes_accessed=moved, transcendentals=0),
        name=name,
    )(*args)


def f32(*shape):
    return jax.ShapeDtypeStruct(shape, jnp.float32)


def far(*shape):
    return pltpu.HBM(shape, jnp.float32)


def gram_kernel(parts, own, gram):
    total = jnp.sum(parts[...], 0)
    own[...] = total
    n = total.shape[1] // 2
    left = dot(total, total[:, :n], ((0,), (0,)))
    right = dot(total[:, n:], total[:, n:], ((0,), (0,)))
    packed = jnp.concatenate([left[:n], left[n:], right], 1)
    gram[...] = packed.reshape(gram.shape)


def tile_kernel(parts, tiles):
    total = jnp.sum(parts[...], 0)
    for i in range(tiles.shape[0]):
        tiles[i] = total


def factor_kernel(shares, out, packed):
    n = out.shape[0] // 2
    packed[...] = shares[...].reshape(packed.shape)
    top = inverse_factor(packed[:, :n])
    low = dot(packed[:, n : 2 * n], top, ((1,), (1,)))
    bottom = inverse_factor(packed[:, 2 * n :] - dot(low, low, ((1,), (1,))))
    out[:n, :n] = top
    out[:n, n:] = jnp.zeros((n, n), jnp.float32)
    out[n:, n:] = bottom
    out[n:, :n] = -dot(bottom, dot(low, top, ((1,), (0,))), ((1,), (0,)))


def members(place, refs):
    count = len(refs)
    size = refs[0].shape[0]
    for k, ref in enumerate(refs):
        member = lax.rem(place + count - k, count)
        yield pl.ds(pl.multiple_of(member * size, size), size), ref


def basis_kernel(scale, place, inverse, *refs):
    blocks, out = refs[:-1], refs[-1]
    for rows, block in members(place[0], blocks):
        out[rows, :] = dot(block[...], inverse[...], ((1,), (1,))) * scale


def solve_kernel(inverse, parts, out):
    total = jnp.sum(parts[...], 0)
    out[...] = dot(inverse[...], total, ((1,), (0,))).reshape(out.shape)


def sketch_kernel(gradients, projection, partial, held, weights, sems):
    copies = [pltpu.make_async_copy(projection, weights, sems.at[0])]
    size = held.shape[0] // PIECES
    for i in range(PIECES):
        part = pl.ds(i * size, size)
        copies.append(
            pltpu.make_async_copy(gradients.at[part], held.at[part], sems.at[i + 1])
        )
    for copy in copies:
        copy.start()
    for copy in copies:
        copy.wait()
    value = jnp.dot(held[...], weights[...], preferred_element_type=jnp.float32)
    partial[...] = value.reshape(partial.shape)


def sketch_blocks(gradients, projection, blocks):
    rows, feats = gradients.shape
    rank = projection.shape[1]
    return pl.pallas_call(
        sketch_kernel,
        out_shape=[
            far(blocks, rows // blocks, rank),
            jax.ShapeDtypeStruct(gradients.shape, gradients.dtype),
        ],
        in_specs=[pl.BlockSpec(memory_space=pltpu.HBM)] * 2,
        out_specs=[pl.BlockSpec(), pl.BlockSpec(memory_space=pltpu.VMEM)],
        scratch_shapes=[
            pltpu.VMEM(projection.shape, projection.dtype),
            pltpu.SemaphoreType.DMA((PIECES + 1,)),
        ],
        compiler_params=pltpu.CompilerParams(vmem_limit_bytes=VMEM_LIMIT),
        cost_estimate=pl.CostEstimate(
            flops=2 * rows * feats * rank,
            bytes_accessed=2 * feats * (rows + rank),
            transcendentals=0,
        ),
        name="sketch",
    )(
        pltpu.with_memory_space_constraint(gradients, pltpu.HBM),
        pltpu.with_memory_space_constraint(projection, pltpu.HBM),
    )


def moment_kernel(place, gradients, *refs):
    half, out = refs[-1], refs[-2]
    blocks, added = refs[:GROUPS], refs[GROUPS:-2]
    for rows, block in members(place[1], blocks):
        half[rows, :] = block[...].astype(half.dtype)
    turned = half[...].T
    count, _, width = out.shape
    for i in range(0, count, 2):
        start = pl.multiple_of((place[0] * count + i) * width, 2 * width)
        value = jnp.dot(
            turned,
            gradients[:, pl.ds(start, 2 * width)],
            preferred_element_type=jnp.float32,
        )
        for j in range(2):
            part = value[:, j * width : (j + 1) * width]
            out[i + j] = part + added[0][i + j] if added else part


def moment_blocks(place, gradients, blocks, count, flops, *added):
    rows, feats = gradients.shape
    rank = blocks[0].shape[1]
    width = feats // (2 * count)
    whole = pl.BlockSpec()
    return pl.pallas_call(
        moment_kernel,
        out_shape=far(count, rank, width),
        in_specs=[
            pl.BlockSpec(memory_space=pltpu.SMEM),
            pl.BlockSpec(memory_space=pltpu.VMEM),
        ]
        + [whole] * (len(blocks) + len(added)),
        out_specs=whole,
        scratch_shapes=[pltpu.VMEM((rows, rank), jnp.bfloat16)],
        compiler_params=pltpu.CompilerParams(vmem_limit_bytes=VMEM_LIMIT),
        cost_estimate=pl.CostEstimate(
            flops=flops,
            bytes_accessed=rows * width * count * 2 + rank * width * count * 4,
            transcendentals=0,
        ),
        name="moment",
    )(place, gradients, *blocks, *added)


def part_kernel(pair, local, away, kept, given):
    count = kept.shape[0]
    for n, out in enumerate((kept, given)):
        rows = pl.ds(lax.rem(pair[0] + n, 2) * count, count)
        out[...] = local[rows] + away[rows]


def add_kernel(a, b, out):
    out[...] = a[...] + b[...]


def on_device(gradients, projection):
    rows, feats = gradients.shape
    rank = projection.shape[1]
    members_of_rows, near = lax.axis_size(ROWS), lax.axis_size(NEAR)
    deep, pairs, xs, cores = (lax.axis_size(a) for a in (DEEP, "pair", "x", "core"))
    scale = float(rows * members_of_rows) ** 0.5
    core = lax.axis_index("core").astype(jnp.int32)
    mine = lax.axis_index("y").astype(jnp.int32)
    share = (rank // 2 // near, 3 * rank // 2)
    width = feats // (cores * pairs * xs)

    with jax.named_scope("sketch"):
        partial, held = sketch_blocks(gradients, projection, GROUPS)
        parts = exchange(partial, "y")

    with jax.named_scope("gram"):
        own, shares = call(
            gram_kernel,
            "gram",
            12 * rows // GROUPS * rank**2,
            [far(rows // GROUPS, rank), far(near, *share)],
            parts,
        )
        shares = exchange(shares, NEAR)

    with jax.named_scope("gather"):
        blocks = [own] + [shifted(own, "y", k) for k in range(1, GROUPS)]
        blocks = [pltpu.with_memory_space_constraint(b, pltpu.HBM) for b in blocks]

    with jax.named_scope("moment"):
        swap = [(0, 1), (1, 0)]
        pair = lax.axis_index("pair").astype(jnp.int32)
        count = pairs * xs
        away = moment_blocks(jnp.stack([1 - core, mine]), held, blocks, count, 10**8)
        away = lax.ppermute(away, "core", swap)
        local = moment_blocks(jnp.stack([core, mine]), held, blocks, count, SHORT)
        local = pltpu.with_memory_space_constraint(local, pltpu.HBM)
        kept, given = call(
            part_kernel, "part", 0, [far(xs, rank, width)] * 2, pair[None], local, away
        )
        given = lax.ppermute(given, "pair", swap)
        (moment,) = call(add_kernel, "add", 0, [far(xs, rank, width)], kept, given)

    with jax.named_scope("gram"):
        (shares,) = call(tile_kernel, "tile", SHORT, [far(deep, *share)], shares)
        shares = exchange(shares, DEEP)
        (shares,) = call(tile_kernel, "tile", SHORT, [far(near, *share)], shares)
        shares = exchange(shares, NEAR)

    with jax.named_scope("moment"):
        moment = exchange(moment, "x")

    with jax.named_scope("factor"):
        (inverse,) = call(
            factor_kernel,
            "factor",
            10**10,
            [f32(rank, rank)],
            shares,
            scratch=[pltpu.VMEM((rank // 2, 3 * rank // 2), jnp.float32)],
        )

    with jax.named_scope("reduced"):
        (parts,) = call(
            solve_kernel,
            "solve",
            12 * rank**2 * width,
            [f32(members_of_rows, rank // members_of_rows, width)],
            inverse,
            moment,
        )
        parts = exchange(parts, ROWS)
        parts = parts.reshape(-1, pairs, xs, cores, rank // members_of_rows, width).sum(0)
        reduced = parts.transpose(3, 2, 0, 1, 4).reshape(rank // members_of_rows, feats)

    with jax.named_scope("basis"):
        (basis,) = call(
            functools.partial(basis_kernel, scale),
            "basis",
            12 * rows * rank**2,
            [f32(rows, rank)],
            mine[None],
            inverse,
            *blocks,
        )
    return (basis, reduced)


def solution(mesh):
    devices = mesh.devices.reshape(8, 2, 4, 2, 4)
    fine = Mesh(devices, ("far", "pair", "x", "core", "y"))
    in_specs = (P(ROWS, "y"), P("y", None))
    out_specs = (P(ROWS, None), P(ROWS, "y"))
    return jax.shard_map(
        on_device, mesh=fine, in_specs=in_specs, out_specs=out_specs, check_vma=False
    )
```

```python
import functools
import math

import jax
import jax.numpy as jnp
from jax import lax
from jax.experimental import pallas as pl
from jax.experimental.pallas import tpu as pltpu
from jax.sharding import Mesh
from jax.sharding import PartitionSpec as P

HIGHEST = lax.Precision.HIGHEST
ROWS = ("far", "pair", "x", "core")
DEEP = ("far", "pair")
CROSS = ("pair", "x")
NEAR = ("x", "core", "y")
GROUPS = 4
PIECES = 4
PANEL = 8
SHORT = 3 * 10**10
VMEM_LIMIT = 8 * 1024 * 1024


def exchange(blocks, axes):
    return lax.all_to_all(blocks, axes, 0, 0)


def shifted(value, axis, by):
    count = lax.axis_size(axis)
    return lax.ppermute(value, axis, [(i, (i + by) % count) for i in range(count)])


def dot(a, b, contract):
    return lax.dot_general(
        a,
        b,
        (contract, ((), ())),
        precision=HIGHEST,
        preferred_element_type=jnp.float32,
    )


def inverse_factor(square):
    n = square.shape[0]
    count = n // PANEL
    sub = lax.broadcasted_iota(jnp.int32, (PANEL, n), 0)
    lane = lax.broadcasted_iota(jnp.int32, (PANEL, n), 1)

    def wide(part):
        return jnp.broadcast_to(part, (PANEL, n))

    left = [square[PANEL * i : PANEL * (i + 1), :] for i in range(count)]
    right = [jnp.where(lane == sub + PANEL * i, 1.0, 0.0) for i in range(count)]
    done = []
    for k in range(count):
        columns = [
            [wide(left[i][:, PANEL * k + j : PANEL * k + j + 1]) for i in range(k, count)]
            for j in range(PANEL)
        ]
        pivots = None
        for j in range(PANEL):
            pivot = wide(columns[j][0][j : j + 1, :])
            pivots = pivot if pivots is None else jnp.where(sub == j, pivot, pivots)
            inverse = 1.0 / pivot
            left_row = wide(left[k][j : j + 1, :])
            right_row = wide(right[k][j : j + 1, :])
            later = [wide(columns[m][0][j : j + 1, :]) for m in range(j + 1, PANEL)]
            for i in range(k, count):
                if i == k and j == PANEL - 1:
                    continue
                scale = columns[j][i - k] * inverse
                if i == k:
                    scale = jnp.where(sub > j, scale, 0.0)
                left[i] = left[i] - scale * left_row
                right[i] = right[i] - scale * right_row
                for m in range(j + 1, PANEL):
                    columns[m][i - k] = columns[m][i - k] - scale * later[m - j - 1]
        done.append(right[k] * lax.rsqrt(pivots))
    return jnp.concatenate(done, 0)


def call(kernel, name, flops, outs, *args, scratch=(), held=True):
    whole = pl.BlockSpec()
    given = pl.BlockSpec(memory_space=pltpu.VMEM) if held else whole
    smem = pl.BlockSpec(memory_space=pltpu.SMEM)
    moved = sum(math.prod(a.shape) * a.dtype.itemsize for a in (*args, *outs))
    return pl.pallas_call(
        kernel,
        out_shape=outs,
        in_specs=[smem if a.ndim == 1 else given for a in args],
        out_specs=[whole] * len(outs),
        scratch_shapes=scratch,
        compiler_params=pltpu.CompilerParams(vmem_limit_bytes=VMEM_LIMIT),
        cost_estimate=pl.CostEstimate(flops=flops, bytes_accessed=moved, transcendentals=0),
        name=name,
    )(*args)


def f32(*shape):
    return jax.ShapeDtypeStruct(shape, jnp.float32)


def far(*shape):
    return pltpu.HBM(shape, jnp.float32)


def gram_kernel(parts, own, gram):
    total = jnp.sum(parts[...], 0)
    own[...] = total
    n = total.shape[1] // 2
    left = dot(total, total[:, :n], ((0,), (0,)))
    right = dot(total[:, n:], total[:, n:], ((0,), (0,)))
    packed = jnp.concatenate([left[:n], left[n:], right], 1)
    gram[...] = packed.reshape(gram.shape)


def tile_kernel(parts, tiles):
    total = jnp.sum(parts[...], 0)
    for i in range(tiles.shape[0]):
        tiles[i] = total


def factor_kernel(shares, out, packed):
    n = out.shape[0] // 2
    packed[...] = shares[...].reshape(packed.shape)
    top = inverse_factor(packed[:, :n])
    low = dot(packed[:, n : 2 * n], top, ((1,), (1,)))
    bottom = inverse_factor(packed[:, 2 * n :] - dot(low, low, ((1,), (1,))))
    out[:n, :n] = top
    out[:n, n:] = jnp.zeros((n, n), jnp.float32)
    out[n:, n:] = bottom
    out[n:, :n] = -dot(bottom, dot(low, top, ((1,), (0,))), ((1,), (0,)))


def members(place, refs):
    count = len(refs)
    size = refs[0].shape[0]
    for k, ref in enumerate(refs):
        member = lax.rem(place + count - k, count)
        yield pl.ds(pl.multiple_of(member * size, size), size), ref


def basis_kernel(scale, place, inverse, *refs):
    blocks, out = refs[:-1], refs[-1]
    for rows, block in members(place[0], blocks):
        out[rows, :] = dot(block[...], inverse[...], ((1,), (1,))) * scale


def solve_kernel(inverse, parts, out):
    total = jnp.sum(parts[...], 0)
    out[...] = dot(inverse[...], total, ((1,), (0,))).reshape(out.shape)


def last_kernel(cores, parts, out):
    width = parts.shape[2]
    count = out.shape[1] // width
    total = jnp.sum(parts[...].reshape(-1, count, *parts.shape[1:]), 0)
    for i in range(count):
        block = i % cores * (count // cores) + i // cores
        out[:, block * width : (block + 1) * width] = total[i]


def sketch_kernel(gradients, projection, partial, held, weights, sems):
    copies = [pltpu.make_async_copy(projection, weights, sems.at[0])]
    size = held.shape[0] // PIECES
    for i in range(PIECES):
        part = pl.ds(i * size, size)
        copies.append(
            pltpu.make_async_copy(gradients.at[part], held.at[part], sems.at[i + 1])
        )
    for copy in copies:
        copy.start()
    for copy in copies:
        copy.wait()
    value = jnp.dot(held[...], weights[...], preferred_element_type=jnp.float32)
    partial[...] = value.reshape(partial.shape)


def sketch_blocks(gradients, projection, blocks):
    rows, feats = gradients.shape
    rank = projection.shape[1]
    return pl.pallas_call(
        sketch_kernel,
        out_shape=[
            f32(blocks, rows // blocks, rank),
            jax.ShapeDtypeStruct(gradients.shape, gradients.dtype),
        ],
        in_specs=[pl.BlockSpec(memory_space=pltpu.HBM)] * 2,
        out_specs=[pl.BlockSpec(), pl.BlockSpec(memory_space=pltpu.VMEM)],
        scratch_shapes=[
            pltpu.VMEM(projection.shape, projection.dtype),
            pltpu.SemaphoreType.DMA((PIECES + 1,)),
        ],
        compiler_params=pltpu.CompilerParams(vmem_limit_bytes=VMEM_LIMIT),
        cost_estimate=pl.CostEstimate(
            flops=2 * rows * feats * rank,
            bytes_accessed=2 * feats * (rows + rank),
            transcendentals=0,
        ),
        name="sketch",
    )(
        pltpu.with_memory_space_constraint(gradients, pltpu.HBM),
        pltpu.with_memory_space_constraint(projection, pltpu.HBM),
    )


def moment_kernel(place, gradients, *refs):
    half, out = refs[-1], refs[-2]
    blocks, added = refs[:GROUPS], refs[GROUPS:-2]
    for rows, block in members(place[1], blocks):
        half[rows, :] = block[...].astype(half.dtype)
    turned = half[...].T
    count, _, width = out.shape
    for i in range(0, count, 2):
        start = pl.multiple_of((place[0] * count + i) * width, 2 * width)
        value = jnp.dot(
            turned,
            gradients[:, pl.ds(start, 2 * width)],
            preferred_element_type=jnp.float32,
        )
        for j in range(2):
            part = value[:, j * width : (j + 1) * width]
            out[i + j] = part + added[0][i + j] if added else part


def moment_blocks(place, gradients, blocks, count, flops, *added):
    rows, feats = gradients.shape
    rank = blocks[0].shape[1]
    width = feats // (2 * count)
    whole = pl.BlockSpec()
    return pl.pallas_call(
        moment_kernel,
        out_shape=far(count, rank, width),
        in_specs=[
            pl.BlockSpec(memory_space=pltpu.SMEM),
            pl.BlockSpec(memory_space=pltpu.VMEM),
        ]
        + [whole] * (len(blocks) + len(added)),
        out_specs=whole,
        scratch_shapes=[pltpu.VMEM((rows, rank), jnp.bfloat16)],
        compiler_params=pltpu.CompilerParams(vmem_limit_bytes=VMEM_LIMIT),
        cost_estimate=pl.CostEstimate(
            flops=flops,
            bytes_accessed=rows * width * count * 2 + rank * width * count * 4,
            transcendentals=0,
        ),
        name="moment",
    )(place, gradients, *blocks, *added)


def on_device(gradients, projection):
    rows, feats = gradients.shape
    rank = projection.shape[1]
    members_of_rows, near = lax.axis_size(ROWS), lax.axis_size(NEAR)
    deep, pairs, xs, cores = (lax.axis_size(a) for a in (DEEP, "pair", "x", "core"))
    scale = float(rows * members_of_rows) ** 0.5
    core = lax.axis_index("core").astype(jnp.int32)
    mine = lax.axis_index("y").astype(jnp.int32)
    share = (rank // 2 // near, 3 * rank // 2)
    width = feats // (cores * pairs * xs)

    with jax.named_scope("sketch"):
        partial, held = sketch_blocks(gradients, projection, GROUPS)
        parts = exchange(partial, "y")

    with jax.named_scope("gram"):
        own, shares = call(
            gram_kernel,
            "gram",
            12 * rows // GROUPS * rank**2,
            [far(rows // GROUPS, rank), far(near, *share)],
            parts,
        )
        shares = exchange(shares, NEAR)
        (shares,) = call(tile_kernel, "tile", SHORT, [far(deep, *share)], shares)
        shares = exchange(shares, DEEP)
        (shares,) = call(tile_kernel, "tile", SHORT, [far(near, *share)], shares)
        shares = exchange(shares, NEAR)

    with jax.named_scope("factor"):
        (inverse,) = call(
            factor_kernel,
            "factor",
            10**10,
            [f32(rank, rank)],
            shares,
            scratch=[pltpu.VMEM((rank // 2, 3 * rank // 2), jnp.float32)],
        )

    with jax.named_scope("gather"):
        blocks = [own] + [shifted(own, "y", k) for k in range(1, GROUPS)]
        blocks = [pltpu.with_memory_space_constraint(b, pltpu.HBM) for b in blocks]

    with jax.named_scope("moment"):
        count = pairs * xs
        away = moment_blocks(jnp.stack([1 - core, mine]), held, blocks, count, SHORT)
        away = lax.ppermute(away, "core", [(0, 1), (1, 0)])
        moment = moment_blocks(
            jnp.stack([core, mine]), held, blocks, count, 10**9, away
        )
        moment = exchange(moment, CROSS)

    with jax.named_scope("reduced"):
        (parts,) = call(
            solve_kernel,
            "solve",
            12 * rank**2 * width,
            [f32(members_of_rows, rank // members_of_rows, width)],
            inverse,
            moment,
        )
        parts = exchange(parts, ROWS)
        (reduced,) = call(
            functools.partial(last_kernel, cores),
            "last",
            0,
            [f32(rank // members_of_rows, feats)],
            parts,
        )

    with jax.named_scope("basis"):
        (basis,) = call(
            functools.partial(basis_kernel, scale),
            "basis",
            12 * rows * rank**2,
            [f32(rows, rank)],
            mine[None],
            inverse,
            *blocks,
            held=False,
        )
    return (basis, reduced)


def solution(mesh):
    devices = mesh.devices.reshape(8, 2, 4, 2, 4)
    fine = Mesh(devices, ("far", "pair", "x", "core", "y"))
    in_specs = (P(ROWS, "y"), P("y", None))
    out_specs = (P(ROWS, None), P(ROWS, "y"))
    return jax.shard_map(
        on_device, mesh=fine, in_specs=in_specs, out_specs=out_specs, check_vma=False
    )
```

```python
import functools
import math

import jax
import jax.numpy as jnp
from jax import lax
from jax.experimental import pallas as pl
from jax.experimental.pallas import tpu as pltpu
from jax.sharding import Mesh
from jax.sharding import PartitionSpec as P

HIGHEST = lax.Precision.HIGHEST
ROWS = ("far", "pair", "x", "core")
DEEP = ("far", "pair")
CROSS = ("pair", "x")
NEAR = ("x", "core", "y")
FIRST = ("pair", *NEAR)
GROUPS = 4
PIECES = 4
PANEL = 8
LONG = 3 * 10**10
VMEM_LIMIT = 8 * 1024 * 1024


def exchange(blocks, axes):
    return lax.all_to_all(blocks, axes, 0, 0)


def shifted(value, axis, by):
    count = lax.axis_size(axis)
    return lax.ppermute(value, axis, [(i, (i + by) % count) for i in range(count)])


def dot(a, b, contract):
    return lax.dot_general(
        a,
        b,
        (contract, ((), ())),
        precision=HIGHEST,
        preferred_element_type=jnp.float32,
    )


def inverse_factor(square):
    n = square.shape[0]
    count = n // PANEL
    sub = lax.broadcasted_iota(jnp.int32, (PANEL, n), 0)
    lane = lax.broadcasted_iota(jnp.int32, (PANEL, n), 1)

    def wide(part):
        return jnp.broadcast_to(part, (PANEL, n))

    left = [square[PANEL * i : PANEL * (i + 1), :] for i in range(count)]
    right = [jnp.where(lane == sub + PANEL * i, 1.0, 0.0) for i in range(count)]
    done = []
    for k in range(count):
        columns = [
            [wide(left[i][:, PANEL * k + j : PANEL * k + j + 1]) for i in range(k, count)]
            for j in range(PANEL)
        ]
        pivots = None
        for j in range(PANEL):
            pivot = wide(columns[j][0][j : j + 1, :])
            pivots = pivot if pivots is None else jnp.where(sub == j, pivot, pivots)
            inverse = 1.0 / pivot
            left_row = wide(left[k][j : j + 1, :])
            right_row = wide(right[k][j : j + 1, :])
            later = [wide(columns[m][0][j : j + 1, :]) for m in range(j + 1, PANEL)]
            for i in range(k, count):
                if i == k and j == PANEL - 1:
                    continue
                scale = columns[j][i - k] * inverse
                if i == k:
                    scale = jnp.where(sub > j, scale, 0.0)
                left[i] = left[i] - scale * left_row
                right[i] = right[i] - scale * right_row
                for m in range(j + 1, PANEL):
                    columns[m][i - k] = columns[m][i - k] - scale * later[m - j - 1]
        done.append(right[k] * lax.rsqrt(pivots))
    return jnp.concatenate(done, 0)


def call(kernel, name, flops, outs, *args, scratch=(), held=True):
    whole = pl.BlockSpec()
    given = pl.BlockSpec(memory_space=pltpu.VMEM) if held else whole
    smem = pl.BlockSpec(memory_space=pltpu.SMEM)
    moved = sum(math.prod(a.shape) * a.dtype.itemsize for a in (*args, *outs))
    return pl.pallas_call(
        kernel,
        out_shape=outs,
        in_specs=[smem if a.ndim == 1 else given for a in args],
        out_specs=[whole] * len(outs),
        scratch_shapes=scratch,
        compiler_params=pltpu.CompilerParams(vmem_limit_bytes=VMEM_LIMIT),
        cost_estimate=pl.CostEstimate(flops=flops, bytes_accessed=moved, transcendentals=0),
        name=name,
    )(*args)


def f32(*shape):
    return jax.ShapeDtypeStruct(shape, jnp.float32)


def far(*shape):
    return pltpu.HBM(shape, jnp.float32)


def gram_kernel(parts, own, gram):
    total = jnp.sum(parts[...], 0)
    own[...] = total
    n = total.shape[1] // 2
    left = dot(total, total[:, :n], ((0,), (0,)))
    right = dot(total[:, n:], total[:, n:], ((0,), (0,)))
    packed = jnp.concatenate([left[:n], left[n:], right], 1)
    pairs, near, size, wide = gram.shape
    packed = packed.reshape(near, pairs * size, wide)
    for i in range(pairs):
        gram[i] = packed[:, i * size : (i + 1) * size]


def tile_kernel(parts, tiles):
    total = jnp.sum(parts[...], 0)
    for i in range(tiles.shape[0]):
        tiles[i] = total


def join_kernel(parts, tiles):
    total = jnp.sum(parts[...], 0)
    pairs, size, _ = total.shape
    for i in range(tiles.shape[0]):
        for j in range(pairs):
            tiles[i, j * size : (j + 1) * size] = total[j]


def factor_kernel(shares, out, packed):
    n = out.shape[0] // 2
    packed[...] = shares[...].reshape(packed.shape)
    top = inverse_factor(packed[:, :n])
    low = dot(packed[:, n : 2 * n], top, ((1,), (1,)))
    bottom = inverse_factor(packed[:, 2 * n :] - dot(low, low, ((1,), (1,))))
    out[:n, :n] = top
    out[:n, n:] = jnp.zeros((n, n), jnp.float32)
    out[n:, n:] = bottom
    out[n:, :n] = -dot(bottom, dot(low, top, ((1,), (0,))), ((1,), (0,)))


def members(place, refs):
    count = len(refs)
    size = refs[0].shape[0]
    for k, ref in enumerate(refs):
        member = lax.rem(place + count - k, count)
        yield pl.ds(pl.multiple_of(member * size, size), size), ref


def basis_kernel(scale, place, inverse, *refs):
    blocks, out = refs[:-1], refs[-1]
    for rows, block in members(place[0], blocks):
        out[rows, :] = dot(block[...], inverse[...], ((1,), (1,))) * scale


def solve_kernel(inverse, parts, out):
    total = jnp.sum(parts[...], 0)
    out[...] = dot(inverse[...], total, ((1,), (0,))).reshape(out.shape)


def last_kernel(cores, parts, out):
    width = parts.shape[2]
    count = out.shape[1] // width
    total = jnp.sum(parts[...].reshape(-1, count, *parts.shape[1:]), 0)
    for i in range(count):
        block = i % cores * (count // cores) + i // cores
        out[:, block * width : (block + 1) * width] = total[i]


def sketch_kernel(gradients, projection, partial, held, weights, sems):
    copies = [pltpu.make_async_copy(projection, weights, sems.at[0])]
    size = held.shape[0] // PIECES
    for i in range(PIECES):
        part = pl.ds(i * size, size)
        copies.append(
            pltpu.make_async_copy(gradients.at[part], held.at[part], sems.at[i + 1])
        )
    for copy in copies:
        copy.start()
    for copy in copies:
        copy.wait()
    value = jnp.dot(held[...], weights[...], preferred_element_type=jnp.float32)
    partial[...] = value.reshape(partial.shape)


def sketch_blocks(gradients, projection, blocks):
    rows, feats = gradients.shape
    rank = projection.shape[1]
    return pl.pallas_call(
        sketch_kernel,
        out_shape=[
            f32(blocks, rows // blocks, rank),
            jax.ShapeDtypeStruct(gradients.shape, gradients.dtype),
        ],
        in_specs=[pl.BlockSpec(memory_space=pltpu.HBM)] * 2,
        out_specs=[pl.BlockSpec(), pl.BlockSpec(memory_space=pltpu.VMEM)],
        scratch_shapes=[
            pltpu.VMEM(projection.shape, projection.dtype),
            pltpu.SemaphoreType.DMA((PIECES + 1,)),
        ],
        compiler_params=pltpu.CompilerParams(vmem_limit_bytes=VMEM_LIMIT),
        cost_estimate=pl.CostEstimate(
            flops=2 * rows * feats * rank,
            bytes_accessed=2 * feats * (rows + rank),
            transcendentals=0,
        ),
        name="sketch",
    )(
        pltpu.with_memory_space_constraint(gradients, pltpu.HBM),
        pltpu.with_memory_space_constraint(projection, pltpu.HBM),
    )


def moment_kernel(place, gradients, *refs):
    half, out = refs[-1], refs[-2]
    blocks, added = refs[:GROUPS], refs[GROUPS:-2]
    for rows, block in members(place[1], blocks):
        half[rows, :] = block[...].astype(half.dtype)
    turned = half[...].T
    count, _, width = out.shape
    for i in range(0, count, 2):
        start = pl.multiple_of((place[0] * count + i) * width, 2 * width)
        value = jnp.dot(
            turned,
            gradients[:, pl.ds(start, 2 * width)],
            preferred_element_type=jnp.float32,
        )
        for j in range(2):
            part = value[:, j * width : (j + 1) * width]
            out[i + j] = part + added[0][i + j] if added else part


def moment_blocks(place, gradients, blocks, count, flops, *added):
    rows, feats = gradients.shape
    rank = blocks[0].shape[1]
    width = feats // (2 * count)
    whole = pl.BlockSpec()
    return pl.pallas_call(
        moment_kernel,
        out_shape=far(count, rank, width),
        in_specs=[
            pl.BlockSpec(memory_space=pltpu.SMEM),
            pl.BlockSpec(memory_space=pltpu.VMEM),
        ]
        + [whole] * (len(blocks) + len(added)),
        out_specs=whole,
        scratch_shapes=[pltpu.VMEM((rows, rank), jnp.bfloat16)],
        compiler_params=pltpu.CompilerParams(vmem_limit_bytes=VMEM_LIMIT),
        cost_estimate=pl.CostEstimate(
            flops=flops,
            bytes_accessed=rows * width * count * 2 + rank * width * count * 4,
            transcendentals=0,
        ),
        name="moment",
    )(place, gradients, *blocks, *added)


def on_device(gradients, projection):
    rows, feats = gradients.shape
    rank = projection.shape[1]
    members_of_rows, near = lax.axis_size(ROWS), lax.axis_size(NEAR)
    deep, pairs, xs, cores = (lax.axis_size(a) for a in (DEEP, "pair", "x", "core"))
    scale = float(rows * members_of_rows) ** 0.5
    core = lax.axis_index("core").astype(jnp.int32)
    mine = lax.axis_index("y").astype(jnp.int32)
    size, wide = rank // 2 // (pairs * near), 3 * rank // 2
    width = feats // (cores * pairs * xs)

    with jax.named_scope("sketch"):
        partial, held = sketch_blocks(gradients, projection, GROUPS)
        parts = exchange(partial, "y")

    with jax.named_scope("gram"):
        own, shares = call(
            gram_kernel,
            "gram",
            12 * rows // GROUPS * rank**2,
            [far(rows // GROUPS, rank), far(pairs, near, size, wide)],
            parts,
        )
        shares = shares.reshape(pairs * near, size, wide)
        shares = exchange(shares, FIRST)
        (shares,) = call(tile_kernel, "tile", LONG, [far(deep, size, wide)], shares)
        shares = exchange(shares, DEEP).reshape(-1, pairs, size, wide)
        (shares,) = call(
            join_kernel, "join", LONG, [far(near, pairs * size, wide)], shares
        )
        shares = exchange(shares, NEAR)

    with jax.named_scope("factor"):
        (inverse,) = call(
            factor_kernel,
            "factor",
            10**10,
            [f32(rank, rank)],
            shares,
            scratch=[pltpu.VMEM((rank // 2, 3 * rank // 2), jnp.float32)],
        )

    with jax.named_scope("gather"):
        blocks = [own] + [shifted(own, "y", k) for k in range(1, GROUPS)]
        blocks = [pltpu.with_memory_space_constraint(b, pltpu.HBM) for b in blocks]

    with jax.named_scope("moment"):
        count = pairs * xs
        away = moment_blocks(jnp.stack([1 - core, mine]), held, blocks, count, LONG)
        away = lax.ppermute(away, "core", [(0, 1), (1, 0)])
        moment = moment_blocks(
            jnp.stack([core, mine]), held, blocks, count, 10**9, away
        )
        moment = exchange(moment, CROSS)

    with jax.named_scope("reduced"):
        (parts,) = call(
            solve_kernel,
            "solve",
            12 * rank**2 * width,
            [f32(members_of_rows, rank // members_of_rows, width)],
            inverse,
            moment,
        )
        parts = exchange(parts, ROWS)
        (reduced,) = call(
            functools.partial(last_kernel, cores),
            "last",
            0,
            [f32(rank // members_of_rows, feats)],
            parts,
        )

    with jax.named_scope("basis"):
        (basis,) = call(
            functools.partial(basis_kernel, scale),
            "basis",
            12 * rows * rank**2,
            [f32(rows, rank)],
            mine[None],
            inverse,
            *blocks,
            held=False,
        )
    return (basis, reduced)


def solution(mesh):
    devices = mesh.devices.reshape(8, 2, 4, 2, 4)
    fine = Mesh(devices, ("far", "pair", "x", "core", "y"))
    in_specs = (P(ROWS, "y"), P("y", None))
    out_specs = (P(ROWS, None), P(ROWS, "y"))
    return jax.shard_map(
        on_device, mesh=fine, in_specs=in_specs, out_specs=out_specs, check_vma=False
    )
```

```python
import functools
import math

import jax
import jax.numpy as jnp
from jax import lax
from jax.experimental import pallas as pl
from jax.experimental.pallas import tpu as pltpu
from jax.sharding import Mesh
from jax.sharding import PartitionSpec as P

HIGHEST = lax.Precision.HIGHEST
ROWS = ("far", "pair", "x", "core")
DEEP = ("far", "pair")
CROSS = ("pair", "x")
NEAR = ("x", "core", "y")
GROUPS = 4
PIECES = 4
PANEL = 8
LONG = 3 * 10**10
VMEM_LIMIT = 8 * 1024 * 1024


def exchange(blocks, axes):
    return lax.all_to_all(blocks, axes, 0, 0)


def shifted(value, axis, by):
    count = lax.axis_size(axis)
    return lax.ppermute(value, axis, [(i, (i + by) % count) for i in range(count)])


def dot(a, b, contract):
    return lax.dot_general(
        a,
        b,
        (contract, ((), ())),
        precision=HIGHEST,
        preferred_element_type=jnp.float32,
    )


def inverse_factor(square):
    n = square.shape[0]
    count = n // PANEL
    sub = lax.broadcasted_iota(jnp.int32, (PANEL, n), 0)
    lane = lax.broadcasted_iota(jnp.int32, (PANEL, n), 1)

    def wide(part):
        return jnp.broadcast_to(part, (PANEL, n))

    left = [square[PANEL * i : PANEL * (i + 1), :] for i in range(count)]
    right = [jnp.where(lane == sub + PANEL * i, 1.0, 0.0) for i in range(count)]
    done = []
    for k in range(count):
        columns = [
            [wide(left[i][:, PANEL * k + j : PANEL * k + j + 1]) for i in range(k, count)]
            for j in range(PANEL)
        ]
        pivots = None
        for j in range(PANEL):
            pivot = wide(columns[j][0][j : j + 1, :])
            pivots = pivot if pivots is None else jnp.where(sub == j, pivot, pivots)
            inverse = 1.0 / pivot
            left_row = wide(left[k][j : j + 1, :])
            right_row = wide(right[k][j : j + 1, :])
            later = [wide(columns[m][0][j : j + 1, :]) for m in range(j + 1, PANEL)]
            for i in range(k, count):
                if i == k and j == PANEL - 1:
                    continue
                scale = columns[j][i - k] * inverse
                if i == k:
                    scale = jnp.where(sub > j, scale, 0.0)
                left[i] = left[i] - scale * left_row
                right[i] = right[i] - scale * right_row
                for m in range(j + 1, PANEL):
                    columns[m][i - k] = columns[m][i - k] - scale * later[m - j - 1]
        done.append(right[k] * lax.rsqrt(pivots))
    return jnp.concatenate(done, 0)


def call(kernel, name, flops, outs, *args, scratch=(), held=True):
    whole = pl.BlockSpec()
    given = pl.BlockSpec(memory_space=pltpu.VMEM) if held else whole
    smem = pl.BlockSpec(memory_space=pltpu.SMEM)
    moved = sum(math.prod(a.shape) * a.dtype.itemsize for a in (*args, *outs))
    return pl.pallas_call(
        kernel,
        out_shape=outs,
        in_specs=[smem if a.ndim == 1 else given for a in args],
        out_specs=[whole] * len(outs),
        scratch_shapes=scratch,
        compiler_params=pltpu.CompilerParams(vmem_limit_bytes=VMEM_LIMIT),
        cost_estimate=pl.CostEstimate(flops=flops, bytes_accessed=moved, transcendentals=0),
        name=name,
    )(*args)


def f32(*shape):
    return jax.ShapeDtypeStruct(shape, jnp.float32)


def far(*shape):
    return pltpu.HBM(shape, jnp.float32)


def gram_kernel(parts, own, gram):
    total = jnp.sum(parts[...], 0)
    own[...] = total
    n = total.shape[1] // 2
    left = dot(total, total[:, :n], ((0,), (0,)))
    right = dot(total[:, n:], total[:, n:], ((0,), (0,)))
    packed = jnp.concatenate([left[:n], left[n:], right], 1)
    gram[...] = packed.reshape(gram.shape)


def tile_kernel(parts, tiles):
    total = jnp.sum(parts[...], 0)
    for i in range(tiles.shape[0]):
        tiles[i] = total


def factor_kernel(shares, out, packed):
    n = out.shape[0] // 2
    packed[...] = shares[...].reshape(packed.shape)
    top = inverse_factor(packed[:, :n])
    low = dot(packed[:, n : 2 * n], top, ((1,), (1,)))
    bottom = inverse_factor(packed[:, 2 * n :] - dot(low, low, ((1,), (1,))))
    out[:n, :n] = top
    out[:n, n:] = jnp.zeros((n, n), jnp.float32)
    out[n:, n:] = bottom
    out[n:, :n] = -dot(bottom, dot(low, top, ((1,), (0,))), ((1,), (0,)))


def members(place, refs):
    count = len(refs)
    size = refs[0].shape[0]
    for k, ref in enumerate(refs):
        member = lax.rem(place + count - k, count)
        yield pl.ds(pl.multiple_of(member * size, size), size), ref


def basis_kernel(scale, place, inverse, *refs):
    blocks, out = refs[:-1], refs[-1]
    for rows, block in members(place[0], blocks):
        out[rows, :] = dot(block[...], inverse[...], ((1,), (1,))) * scale


def solve_kernel(inverse, parts, out):
    total = jnp.sum(parts[...], 0)
    out[...] = dot(inverse[...], total, ((1,), (0,))).reshape(out.shape)


def last_kernel(cores, parts, out):
    width = parts.shape[2]
    count = out.shape[1] // width
    total = jnp.sum(parts[...].reshape(-1, count, *parts.shape[1:]), 0)
    for i in range(count):
        block = i % cores * (count // cores) + i // cores
        out[:, block * width : (block + 1) * width] = total[i]


def sketch_kernel(gradients, projection, partial, held, weights, sems):
    copies = [pltpu.make_async_copy(projection, weights, sems.at[0])]
    size = held.shape[0] // PIECES
    for i in range(PIECES):
        part = pl.ds(i * size, size)
        copies.append(
            pltpu.make_async_copy(gradients.at[part], held.at[part], sems.at[i + 1])
        )
    for copy in copies:
        copy.start()
    for copy in copies:
        copy.wait()
    value = jnp.dot(held[...], weights[...], preferred_element_type=jnp.float32)
    partial[...] = value.reshape(partial.shape)


def sketch_blocks(gradients, projection, blocks):
    rows, feats = gradients.shape
    rank = projection.shape[1]
    return pl.pallas_call(
        sketch_kernel,
        out_shape=[
            f32(blocks, rows // blocks, rank),
            jax.ShapeDtypeStruct(gradients.shape, gradients.dtype),
        ],
        in_specs=[pl.BlockSpec(memory_space=pltpu.HBM)] * 2,
        out_specs=[pl.BlockSpec(memory_space=pltpu.VMEM)] * 2,
        scratch_shapes=[
            pltpu.VMEM(projection.shape, projection.dtype),
            pltpu.SemaphoreType.DMA((PIECES + 1,)),
        ],
        compiler_params=pltpu.CompilerParams(vmem_limit_bytes=VMEM_LIMIT),
        cost_estimate=pl.CostEstimate(
            flops=2 * rows * feats * rank,
            bytes_accessed=2 * feats * (rows + rank),
            transcendentals=0,
        ),
        name="sketch",
    )(
        pltpu.with_memory_space_constraint(gradients, pltpu.HBM),
        pltpu.with_memory_space_constraint(projection, pltpu.HBM),
    )


def moment_kernel(place, gradients, *refs):
    half, out = refs[-1], refs[-2]
    blocks, added = refs[:GROUPS], refs[GROUPS:-2]
    for rows, block in members(place[1], blocks):
        half[rows, :] = block[...].astype(half.dtype)
    turned = half[...].T
    count, _, width = out.shape
    for i in range(0, count, 2):
        start = pl.multiple_of((place[0] * count + i) * width, 2 * width)
        value = jnp.dot(
            turned,
            gradients[:, pl.ds(start, 2 * width)],
            preferred_element_type=jnp.float32,
        )
        for j in range(2):
            part = value[:, j * width : (j + 1) * width]
            out[i + j] = part + added[0][i + j] if added else part


def moment_blocks(place, gradients, blocks, count, flops, *added):
    rows, feats = gradients.shape
    rank = blocks[0].shape[1]
    width = feats // (2 * count)
    whole = pl.BlockSpec()
    return pl.pallas_call(
        moment_kernel,
        out_shape=far(count, rank, width),
        in_specs=[
            pl.BlockSpec(memory_space=pltpu.SMEM),
            pl.BlockSpec(memory_space=pltpu.VMEM),
        ]
        + [whole] * (len(blocks) + len(added)),
        out_specs=whole,
        scratch_shapes=[pltpu.VMEM((rows, rank), jnp.bfloat16)],
        compiler_params=pltpu.CompilerParams(vmem_limit_bytes=VMEM_LIMIT),
        cost_estimate=pl.CostEstimate(
            flops=flops,
            bytes_accessed=rows * width * count * 2 + rank * width * count * 4,
            transcendentals=0,
        ),
        name="moment",
    )(place, gradients, *blocks, *added)


def on_device(gradients, projection):
    rows, feats = gradients.shape
    rank = projection.shape[1]
    members_of_rows, near = lax.axis_size(ROWS), lax.axis_size(NEAR)
    deep, pairs, xs, cores = (lax.axis_size(a) for a in (DEEP, "pair", "x", "core"))
    scale = float(rows * members_of_rows) ** 0.5
    core = lax.axis_index("core").astype(jnp.int32)
    mine = lax.axis_index("y").astype(jnp.int32)
    share = (rank // 2 // near, 3 * rank // 2)
    width = feats // (cores * pairs * xs)

    with jax.named_scope("sketch"):
        partial, held = sketch_blocks(gradients, projection, GROUPS)
        parts = exchange(partial, "y")

    with jax.named_scope("gram"):
        own, shares = call(
            gram_kernel,
            "gram",
            12 * rows // GROUPS * rank**2,
            [far(rows // GROUPS, rank), far(near, *share)],
            parts,
        )
        shares = exchange(shares, NEAR)
        (shares,) = call(tile_kernel, "tile", LONG, [far(deep, *share)], shares)
        shares = exchange(shares, DEEP)
        (shares,) = call(tile_kernel, "tile", LONG, [far(near, *share)], shares)
        shares = exchange(shares, NEAR)

    with jax.named_scope("factor"):
        (inverse,) = call(
            factor_kernel,
            "factor",
            10**10,
            [f32(rank, rank)],
            shares,
            scratch=[pltpu.VMEM((rank // 2, 3 * rank // 2), jnp.float32)],
        )

    with jax.named_scope("gather"):
        blocks = [own] + [shifted(own, "y", k) for k in range(1, GROUPS)]

    with jax.named_scope("moment"):
        count = pairs * xs
        away = moment_blocks(jnp.stack([1 - core, mine]), held, blocks, count, LONG)
        away = lax.ppermute(away, "core", [(0, 1), (1, 0)])
        moment = moment_blocks(
            jnp.stack([core, mine]), held, blocks, count, 10**9, away
        )
        moment = exchange(moment, CROSS)

    with jax.named_scope("reduced"):
        (parts,) = call(
            solve_kernel,
            "solve",
            12 * rank**2 * width,
            [f32(members_of_rows, rank // members_of_rows, width)],
            inverse,
            moment,
        )
        parts = exchange(parts, ROWS)
        (reduced,) = call(
            functools.partial(last_kernel, cores),
            "last",
            0,
            [f32(rank // members_of_rows, feats)],
            parts,
        )

    with jax.named_scope("basis"):
        (basis,) = call(
            functools.partial(basis_kernel, scale),
            "basis",
            12 * rows * rank**2,
            [f32(rows, rank)],
            mine[None],
            inverse,
            *blocks,
            held=False,
        )
    return (basis, reduced)


def solution(mesh):
    devices = mesh.devices.reshape(8, 2, 4, 2, 4)
    fine = Mesh(devices, ("far", "pair", "x", "core", "y"))
    in_specs = (P(ROWS, "y"), P("y", None))
    out_specs = (P(ROWS, None), P(ROWS, "y"))
    return jax.shard_map(
        on_device, mesh=fine, in_specs=in_specs, out_specs=out_specs, check_vma=False
    )
```

```python
import functools
import math

import jax
import jax.numpy as jnp
from jax import lax
from jax.experimental import pallas as pl
from jax.experimental.pallas import tpu as pltpu
from jax.sharding import Mesh
from jax.sharding import PartitionSpec as P

HIGHEST = lax.Precision.HIGHEST
ROWS = ("far", "pair", "x", "core")
DEEP = ("far", "pair")
CROSS = ("pair", "x")
NEAR = ("x", "core", "y")
GROUPS = 4
PIECES = 4
PANEL = 8
LONG = 3 * 10**10
VMEM_LIMIT = 8 * 1024 * 1024


def exchange(blocks, axes):
    return lax.all_to_all(blocks, axes, 0, 0)


def shifted(value, axis, by):
    count = lax.axis_size(axis)
    return lax.ppermute(value, axis, [(i, (i + by) % count) for i in range(count)])


def dot(a, b, contract):
    return lax.dot_general(
        a,
        b,
        (contract, ((), ())),
        precision=HIGHEST,
        preferred_element_type=jnp.float32,
    )


def inverse_factor(square):
    n = square.shape[0]
    count = n // PANEL
    sub = lax.broadcasted_iota(jnp.int32, (PANEL, n), 0)
    lane = lax.broadcasted_iota(jnp.int32, (PANEL, n), 1)

    def wide(part):
        return jnp.broadcast_to(part, (PANEL, n))

    left = [square[PANEL * i : PANEL * (i + 1), :] for i in range(count)]
    right = [jnp.where(lane == sub + PANEL * i, 1.0, 0.0) for i in range(count)]
    done = []
    for k in range(count):
        columns = [
            [wide(left[i][:, PANEL * k + j : PANEL * k + j + 1]) for i in range(k, count)]
            for j in range(PANEL)
        ]
        pivots = None
        for j in range(PANEL):
            pivot = wide(columns[j][0][j : j + 1, :])
            pivots = pivot if pivots is None else jnp.where(sub == j, pivot, pivots)
            inverse = 1.0 / pivot
            left_row = wide(left[k][j : j + 1, :])
            right_row = wide(right[k][j : j + 1, :])
            later = [wide(columns[m][0][j : j + 1, :]) for m in range(j + 1, PANEL)]
            for i in range(k, count):
                if i == k and j == PANEL - 1:
                    continue
                scale = columns[j][i - k] * inverse
                if i == k:
                    scale = jnp.where(sub > j, scale, 0.0)
                left[i] = left[i] - scale * left_row
                right[i] = right[i] - scale * right_row
                for m in range(j + 1, PANEL):
                    columns[m][i - k] = columns[m][i - k] - scale * later[m - j - 1]
        done.append(right[k] * lax.rsqrt(pivots))
    return jnp.concatenate(done, 0)


def call(kernel, name, flops, outs, *args, scratch=(), held=True):
    whole = pl.BlockSpec()
    given = pl.BlockSpec(memory_space=pltpu.VMEM) if held else whole
    smem = pl.BlockSpec(memory_space=pltpu.SMEM)
    moved = sum(math.prod(a.shape) * a.dtype.itemsize for a in (*args, *outs))
    return pl.pallas_call(
        kernel,
        out_shape=outs,
        in_specs=[smem if a.ndim == 1 else given for a in args],
        out_specs=[whole] * len(outs),
        scratch_shapes=scratch,
        compiler_params=pltpu.CompilerParams(vmem_limit_bytes=VMEM_LIMIT),
        cost_estimate=pl.CostEstimate(flops=flops, bytes_accessed=moved, transcendentals=0),
        name=name,
    )(*args)


def f32(*shape):
    return jax.ShapeDtypeStruct(shape, jnp.float32)


def far(*shape):
    return pltpu.HBM(shape, jnp.float32)


def gram_kernel(parts, own, gram):
    total = jnp.sum(parts[...], 0)
    own[...] = total
    n = total.shape[1] // 2
    left = dot(total, total[:, :n], ((0,), (0,)))
    right = dot(total[:, n:], total[:, n:], ((0,), (0,)))
    packed = jnp.concatenate([left[:n], left[n:], right], 1)
    gram[...] = packed.reshape(gram.shape)


def tile_kernel(parts, tiles):
    total = jnp.sum(parts[...], 0)
    for i in range(tiles.shape[0]):
        tiles[i] = total


def factor_kernel(shares, out, packed):
    n = out.shape[0] // 2
    packed[...] = shares[...].reshape(packed.shape)
    top = inverse_factor(packed[:, :n])
    low = dot(packed[:, n : 2 * n], top, ((1,), (1,)))
    bottom = inverse_factor(packed[:, 2 * n :] - dot(low, low, ((1,), (1,))))
    out[:n, :n] = top
    out[:n, n:] = jnp.zeros((n, n), jnp.float32)
    out[n:, n:] = bottom
    out[n:, :n] = -dot(bottom, dot(low, top, ((1,), (0,))), ((1,), (0,)))


def members(place, refs):
    count = len(refs)
    size = refs[0].shape[0]
    for k, ref in enumerate(refs):
        member = lax.rem(place + count - k, count)
        yield pl.ds(pl.multiple_of(member * size, size), size), ref


def basis_kernel(scale, place, inverse, *refs):
    blocks, out = refs[:-1], refs[-1]
    for rows, block in members(place[0], blocks):
        out[rows, :] = dot(block[...], inverse[...], ((1,), (1,))) * scale


def solve_kernel(inverse, parts, out):
    total = jnp.sum(parts[...], 0)
    out[...] = dot(inverse[...], total, ((1,), (0,))).reshape(out.shape)


def last_kernel(cores, parts, out):
    width = parts.shape[2]
    count = out.shape[1] // width
    total = jnp.sum(parts[...].reshape(-1, count, *parts.shape[1:]), 0)
    for i in range(count):
        block = i % cores * (count // cores) + i // cores
        out[:, block * width : (block + 1) * width] = total[i]


def sketch_kernel(gradients, projection, partial, held, weights, sems):
    copies = [pltpu.make_async_copy(projection, weights, sems.at[0])]
    size = held.shape[0] // PIECES
    for i in range(PIECES):
        part = pl.ds(i * size, size)
        copies.append(
            pltpu.make_async_copy(gradients.at[part], held.at[part], sems.at[i + 1])
        )
    for copy in copies:
        copy.start()
    for copy in copies:
        copy.wait()
    value = jnp.dot(held[...], weights[...], preferred_element_type=jnp.float32)
    partial[...] = value.reshape(partial.shape)


def sketch_blocks(gradients, projection, blocks):
    rows, feats = gradients.shape
    rank = projection.shape[1]
    return pl.pallas_call(
        sketch_kernel,
        out_shape=[
            f32(blocks, rows // blocks, rank),
            jax.ShapeDtypeStruct(gradients.shape, gradients.dtype),
        ],
        in_specs=[pl.BlockSpec(memory_space=pltpu.HBM)] * 2,
        out_specs=[pl.BlockSpec(memory_space=pltpu.VMEM)] * 2,
        scratch_shapes=[
            pltpu.VMEM(projection.shape, projection.dtype),
            pltpu.SemaphoreType.DMA((PIECES + 1,)),
        ],
        compiler_params=pltpu.CompilerParams(vmem_limit_bytes=VMEM_LIMIT),
        cost_estimate=pl.CostEstimate(
            flops=2 * rows * feats * rank,
            bytes_accessed=2 * feats * (rows + rank),
            transcendentals=0,
        ),
        name="sketch",
    )(
        pltpu.with_memory_space_constraint(gradients, pltpu.HBM),
        pltpu.with_memory_space_constraint(projection, pltpu.HBM),
    )


def moment_kernel(place, gradients, *refs):
    half, out = refs[-1], refs[-2]
    blocks, added = refs[:GROUPS], refs[GROUPS:-2]
    for rows, block in members(place[1], blocks):
        half[rows, :] = block[...].astype(half.dtype)
    turned = half[...].T
    count, _, width = out.shape
    for i in range(0, count, 2):
        start = pl.multiple_of((place[0] * count + i) * width, 2 * width)
        value = jnp.dot(
            turned,
            gradients[:, pl.ds(start, 2 * width)],
            preferred_element_type=jnp.float32,
        )
        for j in range(2):
            part = value[:, j * width : (j + 1) * width]
            out[i + j] = part + added[0][i + j] if added else part


def moment_blocks(place, gradients, blocks, count, flops, *added):
    rows, feats = gradients.shape
    rank = blocks[0].shape[1]
    width = feats // (2 * count)
    whole = pl.BlockSpec()
    return pl.pallas_call(
        moment_kernel,
        out_shape=far(count, rank, width),
        in_specs=[
            pl.BlockSpec(memory_space=pltpu.SMEM),
            pl.BlockSpec(memory_space=pltpu.VMEM),
        ]
        + [whole] * (len(blocks) + len(added)),
        out_specs=whole,
        scratch_shapes=[pltpu.VMEM((rows, rank), jnp.bfloat16)],
        compiler_params=pltpu.CompilerParams(vmem_limit_bytes=VMEM_LIMIT),
        cost_estimate=pl.CostEstimate(
            flops=flops,
            bytes_accessed=rows * width * count * 2 + rank * width * count * 4,
            transcendentals=0,
        ),
        name="moment",
    )(place, gradients, *blocks, *added)


def on_device(gradients, projection):
    rows, feats = gradients.shape
    rank = projection.shape[1]
    members_of_rows, near = lax.axis_size(ROWS), lax.axis_size(NEAR)
    deep, pairs, xs, cores = (lax.axis_size(a) for a in (DEEP, "pair", "x", "core"))
    scale = float(rows * members_of_rows) ** 0.5
    core = lax.axis_index("core").astype(jnp.int32)
    mine = lax.axis_index("y").astype(jnp.int32)
    share = (rank // 2 // near, 3 * rank // 2)
    width = feats // (cores * pairs * xs)

    with jax.named_scope("sketch"):
        partial, held = sketch_blocks(gradients, projection, GROUPS)
        parts = exchange(partial, "y")

    with jax.named_scope("gram"):
        own, shares = call(
            gram_kernel,
            "gram",
            12 * rows // GROUPS * rank**2,
            [far(rows // GROUPS, rank), far(near, *share)],
            parts,
        )
        shares = exchange(shares, NEAR)
        (shares,) = call(tile_kernel, "tile", LONG, [far(deep, *share)], shares)
        shares = exchange(shares, DEEP)
        (shares,) = call(tile_kernel, "tile", LONG, [far(near, *share)], shares)
        shares = exchange(shares, NEAR)

    with jax.named_scope("factor"):
        (inverse,) = call(
            factor_kernel,
            "factor",
            10**10,
            [f32(rank, rank)],
            shares,
            scratch=[pltpu.VMEM((rank // 2, 3 * rank // 2), jnp.float32)],
        )

    with jax.named_scope("gather"):
        blocks = [own] + [shifted(own, "y", k) for k in range(1, GROUPS)]
        blocks = [pltpu.with_memory_space_constraint(b, pltpu.HBM) for b in blocks]

    with jax.named_scope("moment"):
        count = pairs * xs
        away = moment_blocks(jnp.stack([1 - core, mine]), held, blocks, count, LONG)
        away = lax.ppermute(away, "core", [(0, 1), (1, 0)])
        moment = moment_blocks(
            jnp.stack([core, mine]), held, blocks, count, 10**9, away
        )
        moment = exchange(moment, CROSS)

    with jax.named_scope("reduced"):
        (parts,) = call(
            solve_kernel,
            "solve",
            12 * rank**2 * width,
            [f32(members_of_rows, rank // members_of_rows, width)],
            inverse,
            moment,
        )
        parts = exchange(parts, ROWS)
        (reduced,) = call(
            functools.partial(last_kernel, cores),
            "last",
            0,
            [f32(rank // members_of_rows, feats)],
            parts,
        )

    with jax.named_scope("basis"):
        (basis,) = call(
            functools.partial(basis_kernel, scale),
            "basis",
            12 * rows * rank**2,
            [f32(rows, rank)],
            mine[None],
            inverse,
            *blocks,
            held=False,
        )
    return (basis, reduced)


def solution(mesh):
    devices = mesh.devices.reshape(8, 2, 4, 2, 4)
    fine = Mesh(devices, ("far", "pair", "x", "core", "y"))
    in_specs = (P(ROWS, "y"), P("y", None))
    out_specs = (P(ROWS, None), P(ROWS, "y"))
    return jax.shard_map(
        on_device, mesh=fine, in_specs=in_specs, out_specs=out_specs, check_vma=False
    )
```

```python
import functools
import math

import jax
import jax.numpy as jnp
from jax import lax
from jax.experimental import pallas as pl
from jax.experimental.pallas import tpu as pltpu
from jax.sharding import Mesh
from jax.sharding import PartitionSpec as P

HIGHEST = lax.Precision.HIGHEST
ROWS = ("far", "pair", "x", "core")
DEEP = ("far", "pair")
CROSS = ("pair", "x")
NEAR = ("x", "core", "y")
GROUPS = 4
PIECES = 8
PANEL = 8
SHORT = 3 * 10**10
VMEM_LIMIT = 8 * 1024 * 1024


def exchange(blocks, axes):
    return lax.all_to_all(blocks, axes, 0, 0)


def shifted(value, axis, by):
    count = lax.axis_size(axis)
    return lax.ppermute(value, axis, [(i, (i + by) % count) for i in range(count)])


def dot(a, b, contract):
    return lax.dot_general(
        a,
        b,
        (contract, ((), ())),
        precision=HIGHEST,
        preferred_element_type=jnp.float32,
    )


def inverse_factor(square):
    n = square.shape[0]
    count = n // PANEL
    sub = lax.broadcasted_iota(jnp.int32, (PANEL, n), 0)
    lane = lax.broadcasted_iota(jnp.int32, (PANEL, n), 1)

    def wide(part):
        return jnp.broadcast_to(part, (PANEL, n))

    left = [square[PANEL * i : PANEL * (i + 1), :] for i in range(count)]
    right = [jnp.where(lane == sub + PANEL * i, 1.0, 0.0) for i in range(count)]
    done = []
    for k in range(count):
        columns = [
            [wide(left[i][:, PANEL * k + j : PANEL * k + j + 1]) for i in range(k, count)]
            for j in range(PANEL)
        ]
        pivots = None
        for j in range(PANEL):
            pivot = wide(columns[j][0][j : j + 1, :])
            pivots = pivot if pivots is None else jnp.where(sub == j, pivot, pivots)
            inverse = 1.0 / pivot
            left_row = wide(left[k][j : j + 1, :])
            right_row = wide(right[k][j : j + 1, :])
            later = [wide(columns[m][0][j : j + 1, :]) for m in range(j + 1, PANEL)]
            for i in range(k, count):
                if i == k and j == PANEL - 1:
                    continue
                scale = columns[j][i - k] * inverse
                if i == k:
                    scale = jnp.where(sub > j, scale, 0.0)
                left[i] = left[i] - scale * left_row
                right[i] = right[i] - scale * right_row
                for m in range(j + 1, PANEL):
                    columns[m][i - k] = columns[m][i - k] - scale * later[m - j - 1]
        done.append(right[k] * lax.rsqrt(pivots))
    return jnp.concatenate(done, 0)


def call(kernel, name, flops, outs, *args, scratch=()):
    whole = pl.BlockSpec()
    smem = pl.BlockSpec(memory_space=pltpu.SMEM)
    moved = sum(math.prod(a.shape) * a.dtype.itemsize for a in (*args, *outs))
    return pl.pallas_call(
        kernel,
        out_shape=outs,
        in_specs=[smem if a.ndim == 1 else whole for a in args],
        out_specs=[whole] * len(outs),
        scratch_shapes=scratch,
        compiler_params=pltpu.CompilerParams(vmem_limit_bytes=VMEM_LIMIT),
        cost_estimate=pl.CostEstimate(flops=flops, bytes_accessed=moved, transcendentals=0),
        name=name,
    )(*args)


def f32(*shape):
    return jax.ShapeDtypeStruct(shape, jnp.float32)


def far(*shape):
    return pltpu.HBM(shape, jnp.float32)


def gram_kernel(parts, own, gram):
    total = jnp.sum(parts[...], 0)
    own[...] = total
    n = total.shape[1] // 2
    left = dot(total, total[:, :n], ((0,), (0,)))
    right = dot(total[:, n:], total[:, n:], ((0,), (0,)))
    packed = jnp.concatenate([left[:n], left[n:], right], 1)
    gram[...] = packed.reshape(gram.shape)


def tile_kernel(parts, tiles):
    total = jnp.sum(parts[...], 0)
    for i in range(tiles.shape[0]):
        tiles[i] = total


def factor_kernel(shares, out, packed):
    n = out.shape[0] // 2
    packed[...] = shares[...].reshape(packed.shape)
    top = inverse_factor(packed[:, :n])
    low = dot(packed[:, n : 2 * n], top, ((1,), (1,)))
    bottom = inverse_factor(packed[:, 2 * n :] - dot(low, low, ((1,), (1,))))
    out[:n, :n] = top
    out[:n, n:] = jnp.zeros((n, n), jnp.float32)
    out[n:, n:] = bottom
    out[n:, :n] = -dot(bottom, dot(low, top, ((1,), (0,))), ((1,), (0,)))


def members(place, refs):
    count = len(refs)
    size = refs[0].shape[0]
    for k, ref in enumerate(refs):
        member = lax.rem(place + count - k, count)
        yield pl.ds(pl.multiple_of(member * size, size), size), ref


def basis_kernel(scale, place, inverse, *refs):
    blocks, out = refs[:-1], refs[-1]
    for rows, block in members(place[0], blocks):
        out[rows, :] = dot(block[...], inverse[...], ((1,), (1,))) * scale


def solve_kernel(inverse, parts, out):
    total = jnp.sum(parts[...], 0)
    out[...] = dot(inverse[...], total, ((1,), (0,))).reshape(out.shape)


def sketch_kernel(gradients, projection, partial, held, weights, sems):
    copies = [pltpu.make_async_copy(projection, weights, sems.at[0])]
    size = held.shape[0] // PIECES
    for i in range(PIECES):
        part = pl.ds(i * size, size)
        copies.append(
            pltpu.make_async_copy(gradients.at[part], held.at[part], sems.at[i + 1])
        )
    for copy in copies:
        copy.start()
    for copy in copies:
        copy.wait()
    value = jnp.dot(held[...], weights[...], preferred_element_type=jnp.float32)
    partial[...] = value.reshape(partial.shape)


def sketch_blocks(gradients, projection, blocks):
    rows, feats = gradients.shape
    rank = projection.shape[1]
    return pl.pallas_call(
        sketch_kernel,
        out_shape=[
            f32(blocks, rows // blocks, rank),
            jax.ShapeDtypeStruct(gradients.shape, gradients.dtype),
        ],
        in_specs=[pl.BlockSpec(memory_space=pltpu.HBM)] * 2,
        out_specs=[pl.BlockSpec(), pl.BlockSpec(memory_space=pltpu.VMEM)],
        scratch_shapes=[
            pltpu.VMEM(projection.shape, projection.dtype),
            pltpu.SemaphoreType.DMA((PIECES + 1,)),
        ],
        compiler_params=pltpu.CompilerParams(vmem_limit_bytes=VMEM_LIMIT),
        cost_estimate=pl.CostEstimate(
            flops=2 * rows * feats * rank,
            bytes_accessed=2 * feats * (rows + rank),
            transcendentals=0,
        ),
        name="sketch",
    )(
        pltpu.with_memory_space_constraint(gradients, pltpu.HBM),
        pltpu.with_memory_space_constraint(projection, pltpu.HBM),
    )


def moment_kernel(place, gradients, *refs):
    half, out = refs[-1], refs[-2]
    blocks, added = refs[:GROUPS], refs[GROUPS:-2]
    for rows, block in members(place[1], blocks):
        half[rows, :] = block[...].astype(half.dtype)
    turned = half[...].T
    count, _, width = out.shape
    for i in range(0, count, 2):
        start = pl.multiple_of((place[0] * count + i) * width, 2 * width)
        value = jnp.dot(
            turned,
            gradients[:, pl.ds(start, 2 * width)],
            preferred_element_type=jnp.float32,
        )
        for j in range(2):
            part = value[:, j * width : (j + 1) * width]
            out[i + j] = part + added[0][i + j] if added else part


def moment_blocks(place, gradients, blocks, count, flops, *added):
    rows, feats = gradients.shape
    rank = blocks[0].shape[1]
    width = feats // (2 * count)
    whole = pl.BlockSpec()
    return pl.pallas_call(
        moment_kernel,
        out_shape=far(count, rank, width),
        in_specs=[
            pl.BlockSpec(memory_space=pltpu.SMEM),
            pl.BlockSpec(memory_space=pltpu.VMEM),
        ]
        + [whole] * (len(blocks) + len(added)),
        out_specs=whole,
        scratch_shapes=[pltpu.VMEM((rows, rank), jnp.bfloat16)],
        compiler_params=pltpu.CompilerParams(vmem_limit_bytes=VMEM_LIMIT),
        cost_estimate=pl.CostEstimate(
            flops=flops,
            bytes_accessed=rows * width * count * 2 + rank * width * count * 4,
            transcendentals=0,
        ),
        name="moment",
    )(place, gradients, *blocks, *added)


def on_device(gradients, projection):
    rows, feats = gradients.shape
    rank = projection.shape[1]
    members_of_rows, near = lax.axis_size(ROWS), lax.axis_size(NEAR)
    deep, pairs, xs, cores = (lax.axis_size(a) for a in (DEEP, "pair", "x", "core"))
    scale = float(rows * members_of_rows) ** 0.5
    core = lax.axis_index("core").astype(jnp.int32)
    mine = lax.axis_index("y").astype(jnp.int32)
    share = (rank // 2 // near, 3 * rank // 2)
    width = feats // (cores * pairs * xs)

    with jax.named_scope("sketch"):
        partial, held = sketch_blocks(gradients, projection, GROUPS)
        parts = exchange(partial, "y")

    with jax.named_scope("gram"):
        own, shares = call(
            gram_kernel,
            "gram",
            12 * rows // GROUPS * rank**2,
            [far(rows // GROUPS, rank), far(near, *share)],
            parts,
        )
        shares = exchange(shares, NEAR)
        (shares,) = call(tile_kernel, "tile", SHORT, [far(deep, *share)], shares)
        shares = exchange(shares, DEEP)
        (shares,) = call(tile_kernel, "tile", SHORT, [far(near, *share)], shares)
        shares = exchange(shares, NEAR)

    with jax.named_scope("factor"):
        (inverse,) = call(
            factor_kernel,
            "factor",
            10**10,
            [f32(rank, rank)],
            shares,
            scratch=[pltpu.VMEM((rank // 2, 3 * rank // 2), jnp.float32)],
        )

    with jax.named_scope("gather"):
        blocks = [own] + [shifted(own, "y", k) for k in range(1, GROUPS)]
        blocks = [pltpu.with_memory_space_constraint(b, pltpu.HBM) for b in blocks]

    with jax.named_scope("moment"):
        count = pairs * xs
        away = moment_blocks(jnp.stack([1 - core, mine]), held, blocks, count, SHORT)
        away = lax.ppermute(away, "core", [(0, 1), (1, 0)])
        moment = moment_blocks(
            jnp.stack([core, mine]), held, blocks, count, 10**9, away
        )
        moment = exchange(moment, CROSS)

    with jax.named_scope("reduced"):
        (parts,) = call(
            solve_kernel,
            "solve",
            12 * rank**2 * width,
            [f32(members_of_rows, rank // members_of_rows, width)],
            inverse,
            moment,
        )
        parts = exchange(parts, ROWS)
        parts = parts.reshape(-1, pairs, xs, cores, rank // members_of_rows, width).sum(0)
        reduced = parts.transpose(3, 2, 0, 1, 4).reshape(rank // members_of_rows, feats)

    with jax.named_scope("basis"):
        (basis,) = call(
            functools.partial(basis_kernel, scale),
            "basis",
            12 * rows * rank**2,
            [f32(rows, rank)],
            mine[None],
            inverse,
            *blocks,
        )
    return (basis, reduced)


def solution(mesh):
    devices = mesh.devices.reshape(8, 2, 4, 2, 4)
    fine = Mesh(devices, ("far", "pair", "x", "core", "y"))
    in_specs = (P(ROWS, "y"), P("y", None))
    out_specs = (P(ROWS, None), P(ROWS, "y"))
    return jax.shard_map(
        on_device, mesh=fine, in_specs=in_specs, out_specs=out_specs, check_vma=False
    )
```
